256 devices in a mesh: seq: 64 (over z, y, core), tp: 4 (over x).
Axes of the slice: x: 4, y: 4, z: 8, core: 2. Of those that a mesh axis runs over, the one named last changes fastest.
Arguments:
- section: bfloat16 [8192, 3072], P('seq'), may hold values from -6 to 6
- history: bfloat16 [16384, 3072], P('seq'), may hold values from -6 to 6
- levels: int32 [256], P('seq'), may hold values from 0 to 3, as said below
- mlp_cached: bfloat16 [8192, 3072], P('seq', 'tp'), may hold values from -3 to 3
- w_qkv: bfloat16 [3, 3072, 1536], P(None, None, 'tp'), may hold values from -4 to 4
- w_out: bfloat16 [1536, 3072], P(None, 'tp'), may hold values from -0.15625 to 0.15625
- modulation: float32 [3, 3072], replicated, may hold values from -3 to 3
- level_embed: float32 [4, 3072], replicated, may hold values from -4 to 4
Outputs:
- out: bfloat16 [8192, 3072], P('seq', 'tp')
The draws below stay inside these ranges and needn't reach their ends.
Inputs may be any that keep to these rules, and one draw needn't show every extreme that they name: `levels`: level l means a kernel of 2^(l+1) tokens. The 4 frames of one device of seq (frames 4*i to 4*i + 3) give at most 64 context rows together, and in every draw some device gives exactly 64.
All inputs are finite; a program needn't handle non-finite values.
Results may differ from the reference program's by a relative error of at most 0.008.
Values may be sent and summed in bfloat16 or wider, within the bound.
No kernel may reach another device: no remote copies, remote signals or barrier semaphores. Data moves between devices by JAX's collectives and lax.ppermute only.
A program may use at most 128 MiB of HBM per device.

```python
import math
import jax
import jax.numpy as jnp
import numpy as np
from jax import lax

D = 3072
HEADS = 12
HD = 128
FT = 64
HF_DEV = 4
SECTION = 8192
HIST_FRAMES = 256


def draw_levels(key, part):
    key = jax.random.fold_in(key, 11)
    device_count = HIST_FRAMES // HF_DEV
    pattern_table = jnp.array(np.array([[0, 1, 2, 2], [1, 2, 3, 3], [2, 2, 3, 3], [1, 1, 2, 3], [0, 2, 3, 3]], np.int32))
    kind_key, heavy_key, roll_key = jax.random.split(key, 3)
    kind_draw = jax.random.randint(kind_key, (device_count,), 0, 5)
    heavy_device = jax.random.randint(heavy_key, (), 0, device_count)
    kind_draw = jnp.where(jnp.arange(device_count) == heavy_device, 0, kind_draw)
    turn_amount = jax.random.randint(roll_key, (device_count, 1), 0, HF_DEV)
    position_map = (jnp.arange(HF_DEV)[None, :] + turn_amount) % HF_DEV
    chosen_rows = pattern_table[kind_draw]
    rolled_rows = jnp.take_along_axis(chosen_rows, position_map, axis=1)
    return rolled_rows.reshape(HIST_FRAMES).astype(jnp.int32)


def draw_w_qkv(key, part):
    key = jax.random.fold_in(key, 23)
    shape_everything = (3, D, HEADS * HD)
    entries = jax.random.normal(key, shape_everything, jnp.float32)
    entries = jnp.clip(entries, -6.0, 6.0) / math.sqrt(D)
    part_scale = jnp.array([1.0, 2.5, 1.0], jnp.float32)[:, None, None]
    return (entries * part_scale).astype(jnp.bfloat16)


def draw_section(key, part):
    key = jax.random.fold_in(key, 37)
    entries = jax.random.normal(key, (SECTION, D), jnp.float32)
    return jnp.clip(entries, -6.0, 6.0).astype(jnp.bfloat16)


def level_of(own_key, extent, shards, low, largest):
    factor_of = 1.0
    for dim, parts in shards:
        steps = jax.random.uniform(jax.random.fold_in(jax.random.fold_in(own_key, 6), dim), (parts,), jnp.float32, low / len(shards), largest / len(shards))
        factor_of = factor_of * jnp.repeat(jnp.exp(steps), extent[dim] // parts).reshape((-1,) + (1,) * (len(extent) - 1 - dim))
    return factor_of


def gaussian(own_key, shape, scale, limit, cuts=(), kind=jnp.bfloat16):
    values = scale * jax.random.normal(own_key, shape, jnp.float32)
    if cuts:
        values = values * level_of(own_key, shape, cuts, -0.22, 0.18)
    return jnp.clip(values, -limit, limit).astype(kind)


def setup_inputs(seed: int = 0) -> dict:
    seeds = jax.random.split(jax.random.key(seed), 9)
    return {
        "section": draw_section(jax.random.fold_in(seeds[8], 71), 0),
        "history": gaussian(seeds[1], (HIST_FRAMES * FT, D), 1.0, 6.0, ((0, 64),)),
        "levels": draw_levels(jax.random.fold_in(seeds[8], 71), 0),
        "mlp_cached": gaussian(seeds[3], (SECTION, D), 0.5, 3.0, ((0, 64), (1, 4))),
        "w_qkv": draw_w_qkv(jax.random.fold_in(seeds[8], 71), 0),
        "w_out": gaussian(seeds[5], (HEADS * HD, D), (HEADS * HD) ** -0.5, 0.15625, ((1, 4),)),
        "modulation": gaussian(seeds[6], (3, D), 0.5, 3.0, (), jnp.float32),
        "level_embed": gaussian(seeds[7], (4, D), 1.0, 4.0, (), jnp.float32),
    }


def modulated_norm(row_block, shift_row, scale_row):
    row_mean = lax.optimization_barrier(jnp.mean(row_block, axis=-1, keepdims=True))
    centred = row_block - row_mean
    spread = lax.optimization_barrier(jnp.mean(centred * centred, axis=-1, keepdims=True))
    return (centred * lax.rsqrt(spread + 1e-06) * (1.0 + scale_row) + shift_row).astype(jnp.bfloat16)

def kernel_sizes(levels):
    kernels = jnp.zeros(levels.shape, jnp.int32)
    for level_id in range(4):
        kernels = kernels + jnp.where(levels == level_id, 2 ** (level_id + 1), 0).astype(jnp.int32)
    return kernels

def level_terms(levels, level_embed):
    terms = jnp.zeros((levels.shape[0], level_embed.shape[1]), jnp.float32)
    for level_id in range(4):
        terms = terms + jnp.where(levels[:, None] == level_id, level_embed[level_id][None, :], 0.0)
    return terms

def reference(section, history, levels, mlp_cached, w_qkv, w_out, modulation, level_embed):
    shift_row, scale_row, gate_row = (modulation[0], modulation[1], modulation[2])
    history_frames = history.reshape(HIST_FRAMES, FT, D).astype(jnp.float32)
    kernels = kernel_sizes(levels)
    slot_index = jnp.arange(FT // 2, dtype=jnp.int32)[None, :, None]
    source_index = jnp.arange(FT, dtype=jnp.int32)[None, None, :]
    kernel_width = kernels[:, None, None]
    in_window = (source_index // kernel_width == slot_index) & (slot_index < FT // kernel_width)
    pooling_factors = jnp.where(in_window, 1.0, 0.0) / kernel_width.astype(jnp.float32)
    pooled_rows = jnp.einsum('cng,cgu->cnu', pooling_factors, history_frames)
    context = pooled_rows + level_terms(levels, level_embed)[:, None, :]
    usable_slot = (slot_index[:, :, 0] < FT // kernels[:, None]).reshape(-1)
    context_per_head = modulated_norm(context.reshape(-1, D), shift_row, scale_row)
    section_h = modulated_norm(section.astype(jnp.float32), shift_row, scale_row)
    queries = jnp.dot(section_h, w_qkv[0], preferred_element_type=jnp.float32).astype(jnp.bfloat16)
    all_rows = jnp.concatenate([section_h, context_per_head], axis=0)
    key_rows = jnp.dot(all_rows, w_qkv[1], preferred_element_type=jnp.float32).astype(jnp.bfloat16)
    value_rows = jnp.dot(all_rows, w_qkv[2], preferred_element_type=jnp.float32).astype(jnp.bfloat16)
    usable = jnp.concatenate([jnp.ones((SECTION,), bool), usable_slot])
    query_block = math.gcd(SECTION, 512)
    per_head = []
    for head_id in range(HEADS):
        head_queries = queries[:, head_id * HD:(head_id + 1) * HD].reshape(SECTION // query_block, query_block, HD)
        head_keys = key_rows[:, head_id * HD:(head_id + 1) * HD]
        head_values = value_rows[:, head_id * HD:(head_id + 1) * HD]

        def attend_block(block_queries):
            scores = jnp.dot(block_queries, head_keys.T, preferred_element_type=jnp.float32) * HD ** (-0.5)
            scores = jnp.where(usable[None, :], scores, -jnp.inf)
            row_max = lax.optimization_barrier(jnp.max(scores, axis=-1, keepdims=True))
            expon = jnp.exp(scores - row_max)
            denominator = lax.optimization_barrier(jnp.sum(expon, axis=-1, keepdims=True))
            return jnp.dot(expon.astype(jnp.bfloat16), head_values, preferred_element_type=jnp.float32) / denominator
        per_head.append(lax.map(attend_block, head_queries).reshape(SECTION, HD))
    attended = jnp.concatenate(per_head, axis=1).astype(jnp.bfloat16)
    projected = jnp.dot(attended, w_out, preferred_element_type=jnp.float32)
    result = section.astype(jnp.float32) + gate_row * (projected + mlp_cached.astype(jnp.float32))
    return result.astype(jnp.bfloat16)
```

```python
import functools
import math

import jax
import jax.numpy as jnp
from jax import lax
from jax.experimental import pallas as pl
from jax.experimental.pallas import tpu as pltpu
from jax.sharding import PartitionSpec as P

HD = 128
HEADS_DEV = 3
WH = HEADS_DEV * HD
D = 3072
ZN, YN, CN, XN = 8, 4, 2, 4
SEC = 128
CTX = 64
ROWS = SEC + CTX
FT = 64
FRAMES = 4
STAT_ROWS = 16
PAD_KEY = 2.0**126
PAD_TEST = 2.0**125
TO_LOG2 = HD**-0.5 * math.log2(math.e)
MIB = 1024 * 1024
PREP_VMEM = 63 * MIB
ATTEND_VMEM = 24 * MIB
SMALL_VMEM = 8 * MIB

f32 = jnp.float32
bf16 = jnp.bfloat16


def norm_rows(rows, shift_row, scale_row):
    row_mean = jnp.mean(rows, axis=-1, keepdims=True)
    centred = rows - row_mean
    spread = jnp.mean(centred * centred, axis=-1, keepdims=True)
    return (centred * lax.rsqrt(spread + 1e-06) * (1.0 + scale_row) + shift_row).astype(bf16)


def prep_kernel(
    levels_in, modulation_in, embed_in, section, history, w_qkv,
    key_value, queries,
    levels, modulation, level_embed, sec_buf, hist_buf, w_buf, pooled, rows_h, sems,
):
    half = D // 2
    spans = [pl.ds(0, half), pl.ds(half, half)]
    copies = [
        pltpu.make_async_copy(levels_in, levels, sems.at[0]),
        pltpu.make_async_copy(modulation_in, modulation, sems.at[1]),
        pltpu.make_async_copy(section, sec_buf, sems.at[2]),
        pltpu.make_async_copy(history, hist_buf, sems.at[3]),
        pltpu.make_async_copy(embed_in, level_embed, sems.at[4]),
    ]
    weight_copies = [
        pltpu.make_async_copy(w_qkv.at[which, spans[part]], w_buf.at[which, spans[part]], sems.at[5 + index])
        for index, (which, part) in enumerate(((1, 0), (2, 0), (1, 1), (2, 1), (0, 0), (0, 1)))
    ]
    for copy in copies + weight_copies:
        copy.start()

    copies[1].wait()
    shift_row = modulation[0:1, :]
    scale_row = modulation[1:2, :]
    copies[2].wait()

    def section_step(step, carry):
        span = pl.ds(pl.multiple_of(step * 16, 16), 16)
        rows_h[span, :] = norm_rows(sec_buf[span, :].astype(f32), shift_row, scale_row)
        return carry

    lax.fori_loop(0, SEC // 16, section_step, 0, unroll=2)

    copies[0].wait()
    counts = []
    starts = []
    total = jnp.int32(0)
    for frame in range(FRAMES):
        starts.append(total)
        counts.append(lax.shift_right_logical(jnp.int32(FT // 2), levels[frame]))
        total = total + counts[frame]

    slot = lax.broadcasted_iota(jnp.int32, (CTX, FRAMES * FT), 0)
    source = lax.broadcasted_iota(jnp.int32, (CTX, FRAMES * FT), 1)
    factors = jnp.zeros((CTX, FRAMES * FT), f32)
    for frame in range(FRAMES):
        width = lax.shift_left(jnp.int32(2), levels[frame])
        first = (slot - starts[frame]) * width + frame * FT
        inside = (
            (source >= first)
            & (source < first + width)
            & (source >= frame * FT)
            & (source < (frame + 1) * FT)
        )
        factors = factors + jnp.where(inside, 1.0 / width.astype(f32), 0.0)
    copies[3].wait()
    pooled[...] = jnp.dot(factors.astype(bf16), hist_buf[...], preferred_element_type=f32)
    copies[4].wait()

    def context_step(step, carry):
        span = pl.ds(pl.multiple_of(step * 16, 16), 16)
        rows = pooled[span, :]
        index = lax.broadcasted_iota(jnp.int32, (16, 1), 0) + step * 16
        for frame in range(FRAMES):
            mine = (index >= starts[frame]) & (index < starts[frame] + counts[frame])
            rows = rows + jnp.where(mine, level_embed[pl.ds(levels[frame], 1), :], 0.0)
        rows_h[pl.ds(pl.multiple_of(SEC + step * 16, 16), 16), :] = norm_rows(
            rows, shift_row, scale_row
        )
        return carry

    lax.fori_loop(0, CTX // 16, context_step, 0, unroll=2)

    sums = [None, None, None]
    for index, (which, part) in enumerate(((1, 0), (2, 0), (1, 1), (2, 1), (0, 0), (0, 1))):
        weight_copies[index].wait()
        row_count = SEC if which == 0 else ROWS
        piece = jnp.dot(
            rows_h[:row_count, part * half : (part + 1) * half],
            w_buf[which, part * half : (part + 1) * half, :],
            preferred_element_type=f32,
        )
        sums[which] = piece if part == 0 else sums[which] + piece
    row_index = lax.broadcasted_iota(jnp.int32, (ROWS, WH), 0)
    queries[...] = sums[0].astype(bf16)
    key_value[0] = jnp.where(row_index < SEC + total, sums[1], PAD_KEY).astype(bf16)
    key_value[1] = sums[2].astype(bf16)


def prep(section, history, levels, w_qkv, modulation, level_embed):
    any_spec = pl.BlockSpec(memory_space=pl.ANY)
    vmem = pl.BlockSpec(memory_space=pltpu.VMEM)
    return pl.pallas_call(
        prep_kernel,
        out_shape=(
            jax.ShapeDtypeStruct((2, ROWS, WH), bf16),
            jax.ShapeDtypeStruct((SEC, WH), bf16),
        ),
        in_specs=[any_spec] * 6,
        out_specs=(vmem, vmem),
        scratch_shapes=[
            pltpu.SMEM((FRAMES,), jnp.int32),
            pltpu.VMEM((3, D), f32),
            pltpu.VMEM((4, D), f32),
            pltpu.VMEM((SEC, D), bf16),
            pltpu.VMEM((FRAMES * FT, D), bf16),
            pltpu.VMEM((3, D, WH), bf16),
            pltpu.VMEM((CTX, D), f32),
            pltpu.VMEM((ROWS, D), bf16),
            pltpu.SemaphoreType.DMA((11,)),
        ],
        compiler_params=pltpu.CompilerParams(vmem_limit_bytes=PREP_VMEM),
        cost_estimate=pl.CostEstimate(
            flops=2 * ROWS * D * 3 * WH, bytes_accessed=12_000_000, transcendentals=0
        ),
        name="prep",
    )(levels, modulation, level_embed, section, history, w_qkv)


def attend_kernel(block_shapes, first, last, *refs):
    refs = list(refs)
    query_refs = [refs.pop(0) for _ in range(YN)]
    blocks = []
    for joint in block_shapes:
        if joint:
            ref = refs.pop(0)
            blocks.append((ref.at[0], ref.at[1]))
        else:
            key_ref = refs.pop(0)
            blocks.append((key_ref, refs.pop(0)))
    if not first:
        max_in, den_in, num_in = refs.pop(0), refs.pop(0), refs.pop(0)
    outs = refs
    pad = [
        key_ref[SEC:ROWS, 0:1].astype(f32) > PAD_TEST for key_ref, _ in blocks
    ]
    for head in range(HEADS_DEV):
        cols = slice(head * HD, (head + 1) * HD)
        for pair in range(YN // 2):
            lanes = slice(pair * 2 * SEC, (pair + 1) * 2 * SEC)
            query = jnp.concatenate(
                [query_refs[2 * pair][:, cols], query_refs[2 * pair + 1][:, cols]], axis=0
            )
            scores = []
            for (key_ref, _), pad_rows in zip(blocks, pad):
                score = (
                    lax.dot_general(
                        key_ref[:, cols], query, (((1,), (1,)), ((), ())),
                        preferred_element_type=f32,
                    )
                    * TO_LOG2
                )
                scores.append(score[:SEC])
                scores.append(jnp.where(pad_rows, -1e30, score[SEC:]))
            new_max = functools.reduce(
                jnp.maximum, [jnp.max(score, axis=0, keepdims=True) for score in scores]
            )
            if not first:
                old_max = max_in[head : head + 1, lanes]
                new_max = jnp.maximum(new_max, old_max)
                rescale = jnp.exp2(old_max - new_max)
                denominator = den_in[head : head + 1, lanes] * rescale
                numerator = num_in[cols, lanes] * rescale
            else:
                denominator = jnp.zeros((1, 2 * SEC), f32)
                numerator = jnp.zeros((HD, 2 * SEC), f32)
            for index, (_, value_ref) in enumerate(blocks):
                expon = [
                    jnp.exp2(score - new_max) for score in scores[2 * index : 2 * index + 2]
                ]
                for part in expon:
                    denominator = denominator + jnp.sum(part, axis=0, keepdims=True)
                weights = jnp.concatenate([part.astype(bf16) for part in expon], axis=0)
                numerator = numerator + lax.dot_general(
                    value_ref[:, cols], weights, (((0,), (0,)), ((), ())),
                    preferred_element_type=f32,
                )
            if not last:
                outs[0][head : head + 1, lanes] = new_max
                outs[1][head : head + 1, lanes] = denominator
                outs[2][cols, lanes] = numerator
            else:
                local_out = (numerator / denominator).astype(bf16)
                stat = new_max + jnp.log2(denominator)
                high = stat.astype(bf16).astype(f32)
                middle = (stat - high).astype(bf16).astype(f32)
                low = stat - high - middle
                for half in range(2):
                    piece = slice(half * SEC, (half + 1) * SEC)
                    out = outs[2 * pair + half]
                    out[cols, :] = local_out[:, piece]
                    block = jnp.concatenate(
                        [high[:, piece], middle[:, piece], low[:, piece]], axis=0
                    )
                    stats_ref = outs[YN + 2 * pair + half]
                    stats_ref[head * 3 : head * 3 + 3, :] = block
    if last:
        for index in range(YN):
            stats_ref = outs[YN + index]
            stats_ref[3 * HEADS_DEV : STAT_ROWS, :] = jnp.zeros(
                (STAT_ROWS - 3 * HEADS_DEV, SEC), f32
            )
            outs[index][WH : WH + STAT_ROWS, :] = stats_ref[...].astype(bf16)


def attend(queries, blocks, state, last):
    vmem = pl.BlockSpec(memory_space=pltpu.VMEM)
    block_shapes = tuple(not isinstance(block, tuple) for block in blocks)
    flat = []
    for block in blocks:
        flat.extend(block if isinstance(block, tuple) else (block,))
    operands = list(queries) + flat + (list(state) if state is not None else [])
    count = len(blocks)
    if last:
        out_shape = tuple(
            jax.ShapeDtypeStruct((WH + STAT_ROWS, SEC), bf16) for _ in range(YN)
        )
        scratch = [pltpu.VMEM((STAT_ROWS, SEC), f32) for _ in range(YN)]
    else:
        out_shape = (
            jax.ShapeDtypeStruct((HEADS_DEV, YN * SEC), f32),
            jax.ShapeDtypeStruct((HEADS_DEV, YN * SEC), f32),
            jax.ShapeDtypeStruct((WH, YN * SEC), f32),
        )
        scratch = []
    return pl.pallas_call(
        functools.partial(attend_kernel, block_shapes, state is None, last),
        out_shape=out_shape,
        in_specs=[vmem] * len(operands),
        out_specs=tuple([vmem] * len(out_shape)),
        scratch_shapes=scratch,
        compiler_params=pltpu.CompilerParams(vmem_limit_bytes=ATTEND_VMEM),
        cost_estimate=pl.CostEstimate(
            flops=4 * count * ROWS * YN * SEC * WH,
            bytes_accessed=count * ROWS * WH * 4 + 2_000_000,
            transcendentals=count * ROWS * YN * SEC * HEADS_DEV,
        ),
        name="attend",
    )(*operands)


def merge_kernel(*refs):
    parts, out = refs[:YN], refs[YN]
    for head in range(HEADS_DEV):
        cols = slice(head * HD, (head + 1) * HD)
        stats = []
        for part in parts:
            block = part[WH : WH + STAT_ROWS, :].astype(f32)
            stats.append(
                block[3 * head : 3 * head + 1]
                + block[3 * head + 1 : 3 * head + 2]
                + block[3 * head + 2 : 3 * head + 3]
            )
        top = functools.reduce(jnp.maximum, stats)
        shares = [jnp.exp2(stat - top) for stat in stats]
        whole = functools.reduce(jnp.add, shares)
        total = functools.reduce(
            jnp.add, [part[cols, :].astype(f32) * share for part, share in zip(parts, shares)]
        )
        out[:, cols] = jnp.transpose(total / whole).astype(bf16)


def merge(parts):
    vmem = pl.BlockSpec(memory_space=pltpu.VMEM)
    return pl.pallas_call(
        merge_kernel,
        out_shape=jax.ShapeDtypeStruct((SEC, WH), bf16),
        in_specs=[vmem] * YN,
        out_specs=vmem,
        compiler_params=pltpu.CompilerParams(vmem_limit_bytes=SMALL_VMEM),
        cost_estimate=pl.CostEstimate(flops=500_000, bytes_accessed=500_000, transcendentals=0),
        name="merge",
    )(*parts)


def finish_kernel(place, *refs):
    pieces = refs[:XN]
    w_out, section, gate, mlp, out = refs[XN:]
    me = place[0]
    total = None
    for shift, piece in enumerate(pieces):
        owner = lax.rem(me - shift + XN, XN)
        rows = w_out[pl.ds(pl.multiple_of(owner * WH, WH), WH), :]
        product = jnp.dot(piece[...], rows, preferred_element_type=f32)
        total = product if total is None else total + product
    width = out.shape[1]
    cols = pl.ds(pl.multiple_of(me * width, width), width)
    out[...] = (
        section[:, cols].astype(f32) + gate[2:3, cols] * (total + mlp[...].astype(f32))
    ).astype(bf16)


def finish(place, pieces, w_out, section, modulation, mlp_cached):
    vmem = pl.BlockSpec(memory_space=pltpu.VMEM)
    return pl.pallas_call(
        finish_kernel,
        out_shape=jax.ShapeDtypeStruct(mlp_cached.shape, bf16),
        in_specs=[pl.BlockSpec(memory_space=pltpu.SMEM)] + [vmem] * (XN + 4),
        out_specs=vmem,
        compiler_params=pltpu.CompilerParams(vmem_limit_bytes=SMALL_VMEM),
        cost_estimate=pl.CostEstimate(
            flops=2 * SEC * XN * WH * 768, bytes_accessed=4_000_000, transcendentals=0
        ),
        name="finish",
    )(place, *pieces, w_out, section, modulation, mlp_cached)


def seq_shift(array, dz, dy, dc):
    pairs = []
    for z in range(ZN):
        for y in range(YN):
            for c in range(CN):
                source = (z * YN + y) * CN + c
                target = ((z + dz) % ZN * YN + (y + dy) % YN) * CN + (c + dc) % CN
                pairs.append((source, target))
    return lax.ppermute(array, "seq", pairs)


def tp_shift(array, dx):
    return lax.ppermute(array, "tp", [(x, (x + dx) % XN) for x in range(XN)])


def local(section, history, levels, mlp_cached, w_qkv, w_out, modulation, level_embed):
    key_value, query = prep(section, history, levels, w_qkv, modulation, level_embed)
    up = seq_shift(key_value, 1, 0, 0)
    down = seq_shift(key_value, -1, 0, 0)
    queries = [query] + [seq_shift(query, 0, dy, 0) for dy in (1, 3, 2)]
    sibling = seq_shift(key_value, 0, 0, 1)
    blocks = [key_value, sibling]
    state = None
    for step in range(3):
        if state is not None:
            up, down, state = lax.optimization_barrier((up, down, state))
        if step < 2:
            next_up = seq_shift(up, 1, 0, 0)
            next_down = seq_shift(down, -1, 0, 0)
        else:
            far_key = seq_shift(up[0], 1, 0, 0)
            far_value = seq_shift(down[1], -1, 0, 0)
        blocks += [up, down, seq_shift(up, 0, 0, 1), seq_shift(down, 0, 0, 1)]
        state = attend(queries, blocks, state, False)
        blocks = []
        up, down = next_up, next_down
    far_key, far_value, state = lax.optimization_barrier((far_key, far_value, state))
    far = [
        (far_key, far_value),
        (seq_shift(far_key, 0, 0, 1), seq_shift(far_value, 0, 0, 1)),
    ]
    parts = attend(queries, far, state, True)
    parts = [parts[0]] + [
        seq_shift(part, 0, -dy, 0) for part, dy in zip(parts[1:], (1, 3, 2))
    ]
    attended = merge(parts)
    pieces = [attended] + [tp_shift(attended, dx) for dx in range(1, XN)]
    place = lax.axis_index("tp").astype(jnp.int32).reshape(1)
    return finish(place, pieces, w_out, section, modulation, mlp_cached)


def solution(mesh):
    return jax.shard_map(
        local,
        mesh=mesh,
        in_specs=(
            P("seq", None),
            P("seq", None),
            P("seq"),
            P("seq", "tp"),
            P(None, None, "tp"),
            P(None, "tp"),
            P(),
            P(),
        ),
        out_specs=P("seq", "tp"),
        check_vma=False,
    )
```

```python
import functools
import math

import jax
import jax.numpy as jnp
from jax import lax
from jax.experimental import pallas as pl
from jax.experimental.pallas import tpu as pltpu
from jax.sharding import PartitionSpec as P

HD = 128
HEADS_DEV = 3
WH = HEADS_DEV * HD
D = 3072
ZN, YN, CN, XN = 8, 4, 2, 4
SEC = 128
CTX = 64
ROWS = SEC + CTX
FT = 64
FRAMES = 4
STAT_ROWS = 16
PAD_KEY = 2.0**126
PAD_TEST = 2.0**125
TO_LOG2 = HD**-0.5 * math.log2(math.e)
MIB = 1024 * 1024
PREP_VMEM = 63 * MIB
ATTEND_VMEM = 24 * MIB
SMALL_VMEM = 8 * MIB

f32 = jnp.float32
bf16 = jnp.bfloat16


def norm_rows(rows, shift_row, scale_row):
    row_mean = jnp.mean(rows, axis=-1, keepdims=True)
    centred = rows - row_mean
    spread = jnp.mean(centred * centred, axis=-1, keepdims=True)
    return (centred * lax.rsqrt(spread + 1e-06) * (1.0 + scale_row) + shift_row).astype(bf16)


def prep_kernel(
    levels_in, modulation_in, embed_in, section, history, w_qkv,
    key_value, queries,
    levels, modulation, level_embed, sec_buf, hist_buf, w_buf, pooled, rows_h, sems,
):
    half = D // 2
    spans = [pl.ds(0, half), pl.ds(half, half)]
    copies = [
        pltpu.make_async_copy(levels_in, levels, sems.at[0]),
        pltpu.make_async_copy(modulation_in, modulation, sems.at[1]),
        pltpu.make_async_copy(section, sec_buf, sems.at[2]),
        pltpu.make_async_copy(history, hist_buf, sems.at[3]),
        pltpu.make_async_copy(embed_in, level_embed, sems.at[4]),
    ]
    weight_copies = [
        pltpu.make_async_copy(w_qkv.at[which, spans[part]], w_buf.at[which, spans[part]], sems.at[5 + index])
        for index, (which, part) in enumerate(((1, 0), (2, 0), (1, 1), (2, 1), (0, 0), (0, 1)))
    ]
    for copy in copies + weight_copies:
        copy.start()

    copies[1].wait()
    shift_row = modulation[0:1, :]
    scale_row = modulation[1:2, :]
    copies[2].wait()

    def section_step(step, carry):
        span = pl.ds(pl.multiple_of(step * 16, 16), 16)
        rows_h[span, :] = norm_rows(sec_buf[span, :].astype(f32), shift_row, scale_row)
        return carry

    lax.fori_loop(0, SEC // 16, section_step, 0, unroll=2)

    copies[0].wait()
    counts = []
    starts = []
    total = jnp.int32(0)
    for frame in range(FRAMES):
        starts.append(total)
        counts.append(lax.shift_right_logical(jnp.int32(FT // 2), levels[frame]))
        total = total + counts[frame]

    slot = lax.broadcasted_iota(jnp.int32, (CTX, FRAMES * FT), 0)
    source = lax.broadcasted_iota(jnp.int32, (CTX, FRAMES * FT), 1)
    factors = jnp.zeros((CTX, FRAMES * FT), f32)
    for frame in range(FRAMES):
        width = lax.shift_left(jnp.int32(2), levels[frame])
        first = (slot - starts[frame]) * width + frame * FT
        inside = (
            (source >= first)
            & (source < first + width)
            & (source >= frame * FT)
            & (source < (frame + 1) * FT)
        )
        factors = factors + jnp.where(inside, 1.0 / width.astype(f32), 0.0)
    copies[3].wait()
    pooled[...] = jnp.dot(factors.astype(bf16), hist_buf[...], preferred_element_type=f32)
    copies[4].wait()

    def context_step(step, carry):
        span = pl.ds(pl.multiple_of(step * 16, 16), 16)
        rows = pooled[span, :]
        index = lax.broadcasted_iota(jnp.int32, (16, 1), 0) + step * 16
        for frame in range(FRAMES):
            mine = (index >= starts[frame]) & (index < starts[frame] + counts[frame])
            rows = rows + jnp.where(mine, level_embed[pl.ds(levels[frame], 1), :], 0.0)
        rows_h[pl.ds(pl.multiple_of(SEC + step * 16, 16), 16), :] = norm_rows(
            rows, shift_row, scale_row
        )
        return carry

    lax.fori_loop(0, CTX // 16, context_step, 0, unroll=2)

    sums = [None, None, None]
    for index, (which, part) in enumerate(((1, 0), (2, 0), (1, 1), (2, 1), (0, 0), (0, 1))):
        weight_copies[index].wait()
        row_count = SEC if which == 0 else ROWS
        piece = jnp.dot(
            rows_h[:row_count, part * half : (part + 1) * half],
            w_buf[which, part * half : (part + 1) * half, :],
            preferred_element_type=f32,
        )
        sums[which] = piece if part == 0 else sums[which] + piece
    row_index = lax.broadcasted_iota(jnp.int32, (ROWS, WH), 0)
    queries[...] = (sums[0] * TO_LOG2).astype(bf16)
    key_value[0] = jnp.where(row_index < SEC + total, sums[1], PAD_KEY).astype(bf16)
    key_value[1] = sums[2].astype(bf16)


def prep(section, history, levels, w_qkv, modulation, level_embed):
    any_spec = pl.BlockSpec(memory_space=pl.ANY)
    vmem = pl.BlockSpec(memory_space=pltpu.VMEM)
    return pl.pallas_call(
        prep_kernel,
        out_shape=(
            jax.ShapeDtypeStruct((2, ROWS, WH), bf16),
            jax.ShapeDtypeStruct((SEC, WH), bf16),
        ),
        in_specs=[any_spec] * 6,
        out_specs=(vmem, vmem),
        scratch_shapes=[
            pltpu.SMEM((FRAMES,), jnp.int32),
            pltpu.VMEM((3, D), f32),
            pltpu.VMEM((4, D), f32),
            pltpu.VMEM((SEC, D), bf16),
            pltpu.VMEM((FRAMES * FT, D), bf16),
            pltpu.VMEM((3, D, WH), bf16),
            pltpu.VMEM((CTX, D), f32),
            pltpu.VMEM((ROWS, D), bf16),
            pltpu.SemaphoreType.DMA((11,)),
        ],
        compiler_params=pltpu.CompilerParams(vmem_limit_bytes=PREP_VMEM),
        cost_estimate=pl.CostEstimate(
            flops=2 * ROWS * D * 3 * WH, bytes_accessed=12_000_000, transcendentals=0
        ),
        name="prep",
    )(levels, modulation, level_embed, section, history, w_qkv)


def stage_kernel(query_in, block_in, query, block, sems):
    copies = [
        pltpu.make_async_copy(query_in, query, sems.at[0]),
        pltpu.make_async_copy(block_in, block, sems.at[1]),
    ]
    for copy in copies:
        copy.start()
    for copy in copies:
        copy.wait()


def stage(query, block):
    any_spec = pl.BlockSpec(memory_space=pl.ANY)
    vmem = pl.BlockSpec(memory_space=pltpu.VMEM)
    return pl.pallas_call(
        stage_kernel,
        out_shape=(
            jax.ShapeDtypeStruct(query.shape, bf16),
            jax.ShapeDtypeStruct(block.shape, bf16),
        ),
        in_specs=[any_spec, any_spec],
        out_specs=(vmem, vmem),
        scratch_shapes=[pltpu.SemaphoreType.DMA((2,))],
        compiler_params=pltpu.CompilerParams(vmem_limit_bytes=SMALL_VMEM),
        cost_estimate=pl.CostEstimate(flops=0, bytes_accessed=800_000, transcendentals=0),
        name="stage",
    )(query, block)


def attend_kernel(block_shapes, first, last, *refs):
    refs = list(refs)
    query_refs = [refs.pop(0) for _ in range(YN)]
    blocks = []
    for joint in block_shapes:
        if joint:
            ref = refs.pop(0)
            blocks.append((ref.at[0], ref.at[1]))
        else:
            key_ref = refs.pop(0)
            blocks.append((key_ref, refs.pop(0)))
    if not first:
        max_in, den_in, num_in = refs.pop(0), refs.pop(0), refs.pop(0)
    outs = refs
    pad = [key_ref[SEC:ROWS, 0:1].astype(f32) > PAD_TEST for key_ref, _ in blocks]

    def all_scores(head, pair):
        cols = slice(head * HD, (head + 1) * HD)
        query = jnp.concatenate(
            [query_refs[2 * pair][:, cols], query_refs[2 * pair + 1][:, cols]], axis=0
        )
        scores = []
        for (key_ref, _), pad_rows in zip(blocks, pad):
            score = lax.dot_general(
                key_ref[:, cols], query, (((1,), (1,)), ((), ())), preferred_element_type=f32
            )
            scores.append(score[:SEC])
            scores.append(jnp.where(pad_rows, -1e30, score[SEC:]))
        return scores

    order = [(head, pair) for head in range(HEADS_DEV) for pair in range(YN // 2)]
    coming = all_scores(*order[0])
    for place, (head, pair) in enumerate(order):
        cols = slice(head * HD, (head + 1) * HD)
        lanes = slice(pair * 2 * SEC, (pair + 1) * 2 * SEC)
        scores = coming
        if place + 1 < len(order):
            coming = all_scores(*order[place + 1])
        if True:
            new_max = functools.reduce(
                jnp.maximum, [jnp.max(score, axis=0, keepdims=True) for score in scores]
            )
            if not first:
                old_max = max_in[head : head + 1, lanes]
                new_max = jnp.maximum(new_max, old_max)
                rescale = jnp.exp2(old_max - new_max)
                denominator = den_in[head : head + 1, lanes] * rescale
                numerator = num_in[cols, lanes] * rescale
            else:
                denominator = jnp.zeros((1, 2 * SEC), f32)
                numerator = jnp.zeros((HD, 2 * SEC), f32)
            for index, (_, value_ref) in enumerate(blocks):
                expon = [
                    jnp.exp2(score - new_max) for score in scores[2 * index : 2 * index + 2]
                ]
                for part in expon:
                    denominator = denominator + jnp.sum(part, axis=0, keepdims=True)
                weights = jnp.concatenate([part.astype(bf16) for part in expon], axis=0)
                numerator = numerator + lax.dot_general(
                    value_ref[:, cols], weights, (((0,), (0,)), ((), ())),
                    preferred_element_type=f32,
                )
            if not last:
                outs[0][head : head + 1, lanes] = new_max
                outs[1][head : head + 1, lanes] = denominator
                outs[2][cols, lanes] = numerator
            else:
                local_out = (numerator / denominator).astype(bf16)
                stat = new_max + jnp.log2(denominator)
                high = stat.astype(bf16).astype(f32)
                middle = (stat - high).astype(bf16).astype(f32)
                low = stat - high - middle
                for half in range(2):
                    piece = slice(half * SEC, (half + 1) * SEC)
                    out = outs[2 * pair + half]
                    out[cols, :] = local_out[:, piece]
                    block = jnp.concatenate(
                        [high[:, piece], middle[:, piece], low[:, piece]], axis=0
                    )
                    stats_ref = outs[YN + 2 * pair + half]
                    stats_ref[head * 3 : head * 3 + 3, :] = block
    if last:
        for index in range(YN):
            stats_ref = outs[YN + index]
            stats_ref[3 * HEADS_DEV : STAT_ROWS, :] = jnp.zeros(
                (STAT_ROWS - 3 * HEADS_DEV, SEC), f32
            )
            outs[index][WH : WH + STAT_ROWS, :] = stats_ref[...].astype(bf16)


def attend(queries, blocks, state, last):
    vmem = pl.BlockSpec(memory_space=pltpu.VMEM)
    block_shapes = tuple(not isinstance(block, tuple) for block in blocks)
    flat = []
    for block in blocks:
        flat.extend(block if isinstance(block, tuple) else (block,))
    operands = list(queries) + flat + (list(state) if state is not None else [])
    count = len(blocks)
    if last:
        out_shape = tuple(
            jax.ShapeDtypeStruct((WH + STAT_ROWS, SEC), bf16) for _ in range(YN)
        )
        scratch = [pltpu.VMEM((STAT_ROWS, SEC), f32) for _ in range(YN)]
    else:
        out_shape = (
            jax.ShapeDtypeStruct((HEADS_DEV, YN * SEC), f32),
            jax.ShapeDtypeStruct((HEADS_DEV, YN * SEC), f32),
            jax.ShapeDtypeStruct((WH, YN * SEC), f32),
        )
        scratch = []
    return pl.pallas_call(
        functools.partial(attend_kernel, block_shapes, state is None, last),
        out_shape=out_shape,
        in_specs=[vmem] * len(operands),
        out_specs=tuple([vmem] * len(out_shape)),
        scratch_shapes=scratch,
        compiler_params=pltpu.CompilerParams(vmem_limit_bytes=ATTEND_VMEM),
        cost_estimate=pl.CostEstimate(
            flops=4 * count * ROWS * YN * SEC * WH,
            bytes_accessed=count * ROWS * WH * 4 + 2_000_000,
            transcendentals=count * ROWS * YN * SEC * HEADS_DEV,
        ),
        name="attend",
    )(*operands)


def merge_kernel(*refs):
    parts, out = refs[:YN], refs[YN]
    for head in range(HEADS_DEV):
        cols = slice(head * HD, (head + 1) * HD)
        stats = []
        for part in parts:
            block = part[WH : WH + STAT_ROWS, :].astype(f32)
            stats.append(
                block[3 * head : 3 * head + 1]
                + block[3 * head + 1 : 3 * head + 2]
                + block[3 * head + 2 : 3 * head + 3]
            )
        top = functools.reduce(jnp.maximum, stats)
        shares = [jnp.exp2(stat - top) for stat in stats]
        whole = functools.reduce(jnp.add, shares)
        total = functools.reduce(
            jnp.add, [part[cols, :].astype(f32) * share for part, share in zip(parts, shares)]
        )
        out[:, cols] = jnp.transpose(total / whole).astype(bf16)


def merge(parts):
    vmem = pl.BlockSpec(memory_space=pltpu.VMEM)
    return pl.pallas_call(
        merge_kernel,
        out_shape=jax.ShapeDtypeStruct((SEC, WH), bf16),
        in_specs=[vmem] * YN,
        out_specs=vmem,
        compiler_params=pltpu.CompilerParams(vmem_limit_bytes=SMALL_VMEM),
        cost_estimate=pl.CostEstimate(flops=500_000, bytes_accessed=500_000, transcendentals=0),
        name="merge",
    )(*parts)


def finish_kernel(place, *refs):
    pieces = refs[:XN]
    w_out, section, gate, mlp, out = refs[XN:]
    me = place[0]
    total = None
    for shift, piece in zip((0, 2, 1, 3), pieces):
        owner = lax.rem(me - shift + XN, XN)
        rows = w_out[pl.ds(pl.multiple_of(owner * WH, WH), WH), :]
        product = jnp.dot(piece[...], rows, preferred_element_type=f32)
        total = product if total is None else total + product
    width = out.shape[1]
    cols = pl.ds(pl.multiple_of(me * width, width), width)
    out[...] = (
        section[:, cols].astype(f32) + gate[2:3, cols] * (total + mlp[...].astype(f32))
    ).astype(bf16)


def finish(place, pieces, w_out, section, modulation, mlp_cached):
    vmem = pl.BlockSpec(memory_space=pltpu.VMEM)
    return pl.pallas_call(
        finish_kernel,
        out_shape=jax.ShapeDtypeStruct(mlp_cached.shape, bf16),
        in_specs=[pl.BlockSpec(memory_space=pltpu.SMEM)] + [vmem] * (XN + 4),
        out_specs=vmem,
        compiler_params=pltpu.CompilerParams(vmem_limit_bytes=SMALL_VMEM),
        cost_estimate=pl.CostEstimate(
            flops=2 * SEC * XN * WH * 768, bytes_accessed=4_000_000, transcendentals=0
        ),
        name="finish",
    )(place, *pieces, w_out, section, modulation, mlp_cached)


def seq_send(array, target_of):
    pairs = []
    for z in range(ZN):
        for y in range(YN):
            for c in range(CN):
                tz, ty, tc = target_of(z, y, c)
                target = (tz % ZN * YN + ty % YN) * CN + tc % CN
                pairs.append(((z * YN + y) * CN + c, target))
    return lax.ppermute(array, "seq", pairs)


def ring(array):
    return seq_send(array, lambda z, y, c: (z + 1 - 2 * c, y, c))


def swap(array):
    return seq_send(array, lambda z, y, c: (z, y, c + 1))


def after(array, others):
    return lax.optimization_barrier((array, others))[0]


def y_shift(array, dy):
    return seq_send(array, lambda z, y, c: (z, y + dy, c))


def tp_shift(array, dx):
    return lax.ppermute(array, "tp", [(x, (x + dx) % XN) for x in range(XN)])


def local(section, history, levels, mlp_cached, w_qkv, w_out, modulation, level_embed):
    key_value, query = prep(section, history, levels, w_qkv, modulation, level_embed)
    first, second = [key_value], [swap(key_value)]
    first.append(ring(first[0]))
    second.append(ring(second[0]))
    queries = [y_shift(query, dy) for dy in (2, 1, 3)]
    query, first[0] = stage(query, key_value)
    queries = [query] + queries
    first[1], second[1], _ = lax.optimization_barrier(
        (first[1], second[1], (queries, first[0]))
    )
    first.append(ring(first[1]))
    second.append(ring(second[1]))
    state = attend(queries, [first[0], second[0], first[1], swap(first[1])], None, False)
    for step in (2, 3):
        first[step] = after(first[step], state)
        first.append(ring(first[step]))
        second[step] = after(second[step], state)
        if step == 2:
            second.append(ring(second[step]))
        blocks = [second[step - 1], swap(second[step - 1]), first[step], swap(first[step])]
        state = attend(queries, blocks, state, False)
    first[4] = after(first[4], state)
    state = attend(queries, [second[3], swap(second[3])], state, False)
    parts = attend(queries, [first[4], swap(first[4])], state, True)
    parts = [parts[0]] + [y_shift(part, -dy) for part, dy in zip(parts[1:], (2, 1, 3))]
    attended = merge(parts)
    pieces = [attended] + [tp_shift(attended, dx) for dx in (2, 1, 3)]
    place = lax.axis_index("tp").astype(jnp.int32).reshape(1)
    return finish(place, pieces, w_out, section, modulation, mlp_cached)


def solution(mesh):
    return jax.shard_map(
        local,
        mesh=mesh,
        in_specs=(
            P("seq", None),
            P("seq", None),
            P("seq"),
            P("seq", "tp"),
            P(None, None, "tp"),
            P(None, "tp"),
            P(),
            P(),
        ),
        out_specs=P("seq", "tp"),
        check_vma=False,
    )
```

```python
import functools
import math

import jax
import jax.numpy as jnp
from jax import lax
from jax.experimental import pallas as pl
from jax.experimental.pallas import tpu as pltpu
from jax.sharding import PartitionSpec as P

HD = 128
HEADS_DEV = 3
WH = HEADS_DEV * HD
D = 3072
ZN, YN, CN, XN = 8, 4, 2, 4
SEC = 128
CTX = 64
ROWS = SEC + CTX
FT = 64
FRAMES = 4
STAT_ROWS = 16
PAD_KEY = 2.0**126
PAD_TEST = 2.0**125
TO_LOG2 = HD**-0.5 * math.log2(math.e)
MIB = 1024 * 1024
PREP_VMEM = 63 * MIB
ATTEND_VMEM = 24 * MIB
SMALL_VMEM = 8 * MIB

f32 = jnp.float32
bf16 = jnp.bfloat16


def norm_rows(rows, shift_row, scale_row):
    row_mean = jnp.mean(rows, axis=-1, keepdims=True)
    centred = rows - row_mean
    spread = jnp.mean(centred * centred, axis=-1, keepdims=True)
    return (centred * lax.rsqrt(spread + 1e-06) * (1.0 + scale_row) + shift_row).astype(bf16)


def prep_kernel(
    levels_in, modulation_in, embed_in, section, history, w_qkv,
    key_value, queries,
    levels, modulation, level_embed, sec_buf, hist_buf, w_buf, pooled, rows_h, sems,
):
    half = D // 2
    spans = [pl.ds(0, half), pl.ds(half, half)]
    copies = [
        pltpu.make_async_copy(levels_in, levels, sems.at[0]),
        pltpu.make_async_copy(modulation_in, modulation, sems.at[1]),
        pltpu.make_async_copy(section, sec_buf, sems.at[2]),
        pltpu.make_async_copy(history, hist_buf, sems.at[3]),
        pltpu.make_async_copy(embed_in, level_embed, sems.at[4]),
    ]
    weight_copies = [
        pltpu.make_async_copy(
            w_qkv.at[which, spans[part]],
            w_buf.at[spans[part], pl.ds(place * WH, WH)],
            sems.at[5 + index],
        )
        for index, (which, place, part) in enumerate(
            ((1, 0, 0), (2, 1, 0), (1, 0, 1), (2, 1, 1), (0, 2, 0), (0, 2, 1))
        )
    ]
    for copy in copies + weight_copies:
        copy.start()

    copies[1].wait()
    shift_row = modulation[0:1, :]
    scale_row = modulation[1:2, :]
    copies[2].wait()

    def section_step(step, carry):
        span = pl.ds(pl.multiple_of(step * 16, 16), 16)
        rows_h[span, :] = norm_rows(sec_buf[span, :].astype(f32), shift_row, scale_row)
        return carry

    lax.fori_loop(0, SEC // 16, section_step, 0, unroll=4)

    copies[0].wait()
    counts = []
    starts = []
    total = jnp.int32(0)
    for frame in range(FRAMES):
        starts.append(total)
        counts.append(lax.shift_right_logical(jnp.int32(FT // 2), levels[frame]))
        total = total + counts[frame]

    slot = lax.broadcasted_iota(jnp.int32, (CTX, FRAMES * FT), 0)
    source = lax.broadcasted_iota(jnp.int32, (CTX, FRAMES * FT), 1)
    factors = jnp.zeros((CTX, FRAMES * FT), f32)
    for frame in range(FRAMES):
        width = lax.shift_left(jnp.int32(2), levels[frame])
        first = (slot - starts[frame]) * width + frame * FT
        inside = (
            (source >= first)
            & (source < first + width)
            & (source >= frame * FT)
            & (source < (frame + 1) * FT)
        )
        factors = factors + jnp.where(inside, 1.0 / width.astype(f32), 0.0)
    copies[3].wait()
    pooled[...] = jnp.dot(factors.astype(bf16), hist_buf[...], preferred_element_type=f32)
    copies[4].wait()

    def context_step(step, carry):
        span = pl.ds(pl.multiple_of(step * 16, 16), 16)
        rows = pooled[span, :]
        index = lax.broadcasted_iota(jnp.int32, (16, 1), 0) + step * 16
        for frame in range(FRAMES):
            mine = (index >= starts[frame]) & (index < starts[frame] + counts[frame])
            rows = rows + jnp.where(mine, level_embed[pl.ds(levels[frame], 1), :], 0.0)
        rows_h[pl.ds(pl.multiple_of(SEC + step * 16, 16), 16), :] = norm_rows(
            rows, shift_row, scale_row
        )
        return carry

    lax.fori_loop(0, CTX // 16, context_step, 0, unroll=4)

    both = None
    for part in range(2):
        weight_copies[2 * part].wait()
        weight_copies[2 * part + 1].wait()
        span = slice(part * half, (part + 1) * half)
        piece = jnp.dot(
            rows_h[:, span], w_buf[span, : 2 * WH], preferred_element_type=f32
        )
        both = piece if part == 0 else both + piece
    row_index = lax.broadcasted_iota(jnp.int32, (ROWS, WH), 0)
    key_value[0] = jnp.where(row_index < SEC + total, both[:, :WH], PAD_KEY).astype(bf16)
    key_value[1] = both[:, WH:].astype(bf16)
    total = None
    for part in range(2):
        weight_copies[4 + part].wait()
        span = slice(part * half, (part + 1) * half)
        piece = jnp.dot(
            rows_h[:SEC, span], w_buf[span, 2 * WH :], preferred_element_type=f32
        )
        total = piece if part == 0 else total + piece
    queries[...] = (total * TO_LOG2).astype(bf16)


def prep(section, history, levels, w_qkv, modulation, level_embed):
    any_spec = pl.BlockSpec(memory_space=pl.ANY)
    vmem = pl.BlockSpec(memory_space=pltpu.VMEM)
    return pl.pallas_call(
        prep_kernel,
        out_shape=(
            jax.ShapeDtypeStruct((2, ROWS, WH), bf16),
            jax.ShapeDtypeStruct((SEC, WH), bf16),
        ),
        in_specs=[any_spec] * 6,
        out_specs=(vmem, vmem),
        scratch_shapes=[
            pltpu.SMEM((FRAMES,), jnp.int32),
            pltpu.VMEM((3, D), f32),
            pltpu.VMEM((4, D), f32),
            pltpu.VMEM((SEC, D), bf16),
            pltpu.VMEM((FRAMES * FT, D), bf16),
            pltpu.VMEM((D, 3 * WH), bf16),
            pltpu.VMEM((CTX, D), f32),
            pltpu.VMEM((ROWS, D), bf16),
            pltpu.SemaphoreType.DMA((11,)),
        ],
        compiler_params=pltpu.CompilerParams(vmem_limit_bytes=PREP_VMEM),
        cost_estimate=pl.CostEstimate(
            flops=2 * ROWS * D * 3 * WH, bytes_accessed=12_000_000, transcendentals=0
        ),
        name="prep",
    )(levels, modulation, level_embed, section, history, w_qkv)


def stage_kernel(query_in, block_in, query, block, sems):
    copies = [
        pltpu.make_async_copy(query_in, query, sems.at[0]),
        pltpu.make_async_copy(block_in, block, sems.at[1]),
    ]
    for copy in copies:
        copy.start()
    for copy in copies:
        copy.wait()


def stage(query, block):
    any_spec = pl.BlockSpec(memory_space=pl.ANY)
    vmem = pl.BlockSpec(memory_space=pltpu.VMEM)
    return pl.pallas_call(
        stage_kernel,
        out_shape=(
            jax.ShapeDtypeStruct(query.shape, bf16),
            jax.ShapeDtypeStruct(block.shape, bf16),
        ),
        in_specs=[any_spec, any_spec],
        out_specs=(vmem, vmem),
        scratch_shapes=[pltpu.SemaphoreType.DMA((2,))],
        compiler_params=pltpu.CompilerParams(vmem_limit_bytes=SMALL_VMEM),
        cost_estimate=pl.CostEstimate(flops=0, bytes_accessed=800_000, transcendentals=0),
        name="stage",
    )(query, block)


def attend_kernel(block_shapes, first, last, *refs):
    refs = list(refs)
    query_refs = [refs.pop(0) for _ in range(YN)]
    blocks = []
    for joint in block_shapes:
        if joint:
            ref = refs.pop(0)
            blocks.append((ref.at[0], ref.at[1]))
        else:
            key_ref = refs.pop(0)
            blocks.append((key_ref, refs.pop(0)))
    if not first:
        max_in, den_in, num_in = refs.pop(0), refs.pop(0), refs.pop(0)
    outs = refs
    pad = [key_ref[SEC:ROWS, 0:1].astype(f32) > PAD_TEST for key_ref, _ in blocks]

    def all_scores(head, pair):
        cols = slice(head * HD, (head + 1) * HD)
        query = jnp.concatenate(
            [query_refs[2 * pair][:, cols], query_refs[2 * pair + 1][:, cols]], axis=0
        )
        scores = []
        for (key_ref, _), pad_rows in zip(blocks, pad):
            score = lax.dot_general(
                key_ref[:, cols], query, (((1,), (1,)), ((), ())), preferred_element_type=f32
            )
            scores.append(score[:SEC])
            scores.append(jnp.where(pad_rows, -1e30, score[SEC:]))
        return scores

    order = [(head, pair) for head in range(HEADS_DEV) for pair in range(YN // 2)]
    coming = all_scores(*order[0])
    for place, (head, pair) in enumerate(order):
        cols = slice(head * HD, (head + 1) * HD)
        lanes = slice(pair * 2 * SEC, (pair + 1) * 2 * SEC)
        scores = coming
        if place + 1 < len(order):
            coming = all_scores(*order[place + 1])
        if True:
            new_max = functools.reduce(
                jnp.maximum, [jnp.max(score, axis=0, keepdims=True) for score in scores]
            )
            if not first:
                old_max = max_in[head : head + 1, lanes]
                new_max = jnp.maximum(new_max, old_max)
                rescale = jnp.exp2(old_max - new_max)
                denominator = den_in[head : head + 1, lanes] * rescale
                numerator = num_in[cols, lanes] * rescale
            else:
                denominator = jnp.zeros((1, 2 * SEC), f32)
                numerator = jnp.zeros((HD, 2 * SEC), f32)
            for index, (_, value_ref) in enumerate(blocks):
                expon = [
                    jnp.exp2(score - new_max) for score in scores[2 * index : 2 * index + 2]
                ]
                for part in expon:
                    denominator = denominator + jnp.sum(part, axis=0, keepdims=True)
                weights = jnp.concatenate([part.astype(bf16) for part in expon], axis=0)
                numerator = numerator + lax.dot_general(
                    value_ref[:, cols], weights, (((0,), (0,)), ((), ())),
                    preferred_element_type=f32,
                )
            if not last:
                outs[0][head : head + 1, lanes] = new_max
                outs[1][head : head + 1, lanes] = denominator
                outs[2][cols, lanes] = numerator
            else:
                local_out = (numerator / denominator).astype(bf16)
                stat = new_max + jnp.log2(denominator)
                high = stat.astype(bf16).astype(f32)
                middle = (stat - high).astype(bf16).astype(f32)
                low = stat - high - middle
                for half in range(2):
                    piece = slice(half * SEC, (half + 1) * SEC)
                    out = outs[2 * pair + half]
                    out[cols, :] = local_out[:, piece]
                    block = jnp.concatenate(
                        [high[:, piece], middle[:, piece], low[:, piece]], axis=0
                    )
                    stats_ref = outs[YN + 2 * pair + half]
                    stats_ref[head * 3 : head * 3 + 3, :] = block
    if last:
        for index in range(YN):
            stats_ref = outs[YN + index]
            stats_ref[3 * HEADS_DEV : STAT_ROWS, :] = jnp.zeros(
                (STAT_ROWS - 3 * HEADS_DEV, SEC), f32
            )
            outs[index][WH : WH + STAT_ROWS, :] = stats_ref[...].astype(bf16)


def attend(queries, blocks, state, last):
    vmem = pl.BlockSpec(memory_space=pltpu.VMEM)
    block_shapes = tuple(not isinstance(block, tuple) for block in blocks)
    flat = []
    for block in blocks:
        flat.extend(block if isinstance(block, tuple) else (block,))
    operands = list(queries) + flat + (list(state) if state is not None else [])
    count = len(blocks)
    if last:
        out_shape = tuple(
            jax.ShapeDtypeStruct((WH + STAT_ROWS, SEC), bf16) for _ in range(YN)
        )
        scratch = [pltpu.VMEM((STAT_ROWS, SEC), f32) for _ in range(YN)]
    else:
        out_shape = (
            jax.ShapeDtypeStruct((HEADS_DEV, YN * SEC), f32),
            jax.ShapeDtypeStruct((HEADS_DEV, YN * SEC), f32),
            jax.ShapeDtypeStruct((WH, YN * SEC), f32),
        )
        scratch = []
    return pl.pallas_call(
        functools.partial(attend_kernel, block_shapes, state is None, last),
        out_shape=out_shape,
        in_specs=[vmem] * len(operands),
        out_specs=tuple([vmem] * len(out_shape)),
        scratch_shapes=scratch,
        compiler_params=pltpu.CompilerParams(vmem_limit_bytes=ATTEND_VMEM),
        cost_estimate=pl.CostEstimate(
            flops=4 * count * ROWS * YN * SEC * WH,
            bytes_accessed=count * ROWS * WH * 4 + 2_000_000,
            transcendentals=count * ROWS * YN * SEC * HEADS_DEV,
        ),
        name="attend",
    )(*operands)


def merge_kernel(*refs):
    parts, out = refs[:YN], refs[YN]
    for head in range(HEADS_DEV):
        cols = slice(head * HD, (head + 1) * HD)
        stats = []
        for part in parts:
            block = part[WH : WH + STAT_ROWS, :].astype(f32)
            stats.append(
                block[3 * head : 3 * head + 1]
                + block[3 * head + 1 : 3 * head + 2]
                + block[3 * head + 2 : 3 * head + 3]
            )
        top = functools.reduce(jnp.maximum, stats)
        shares = [jnp.exp2(stat - top) for stat in stats]
        whole = functools.reduce(jnp.add, shares)
        total = functools.reduce(
            jnp.add, [part[cols, :].astype(f32) * share for part, share in zip(parts, shares)]
        )
        out[:, cols] = jnp.transpose(total / whole).astype(bf16)


def merge(parts):
    vmem = pl.BlockSpec(memory_space=pltpu.VMEM)
    return pl.pallas_call(
        merge_kernel,
        out_shape=jax.ShapeDtypeStruct((SEC, WH), bf16),
        in_specs=[vmem] * YN,
        out_specs=vmem,
        compiler_params=pltpu.CompilerParams(vmem_limit_bytes=SMALL_VMEM),
        cost_estimate=pl.CostEstimate(flops=500_000, bytes_accessed=500_000, transcendentals=0),
        name="merge",
    )(*parts)


def owned_rows(w_out, owner):
    return w_out[pl.ds(pl.multiple_of(owner * WH, WH), WH), :]


def begin_kernel(place, piece, w_out, section, modulation, mlp, total, gate):
    me = place[0]
    width = total.shape[1]
    cols = pl.ds(pl.multiple_of(me * width, width), width)
    gate[...] = modulation[2:3, cols]
    product = jnp.dot(piece[...], owned_rows(w_out, me), preferred_element_type=f32)
    total[...] = section[:, cols].astype(f32) + gate[...] * (product + mlp[...].astype(f32))


def begin(place, piece, w_out, section, modulation, mlp_cached):
    vmem = pl.BlockSpec(memory_space=pltpu.VMEM)
    return pl.pallas_call(
        begin_kernel,
        out_shape=(
            jax.ShapeDtypeStruct(mlp_cached.shape, f32),
            jax.ShapeDtypeStruct((1, mlp_cached.shape[1]), f32),
        ),
        in_specs=[pl.BlockSpec(memory_space=pltpu.SMEM)] + [vmem] * 5,
        out_specs=(vmem, vmem),
        compiler_params=pltpu.CompilerParams(vmem_limit_bytes=SMALL_VMEM),
        cost_estimate=pl.CostEstimate(
            flops=2 * SEC * WH * 768, bytes_accessed=4_000_000, transcendentals=0
        ),
        name="begin",
    )(place, piece, w_out, section, modulation, mlp_cached)


def finish_kernel(place, *refs):
    pieces = refs[: XN - 1]
    w_out, base, gate, out = refs[XN - 1 :]
    me = place[0]
    total = None
    for shift, piece in zip((2, 1, 3), pieces):
        rows = owned_rows(w_out, lax.rem(me - shift + XN, XN))
        product = jnp.dot(piece[...], rows, preferred_element_type=f32)
        total = product if total is None else total + product
    out[...] = (base[...] + gate[...] * total).astype(bf16)


def finish(place, pieces, w_out, total, gate):
    vmem = pl.BlockSpec(memory_space=pltpu.VMEM)
    return pl.pallas_call(
        finish_kernel,
        out_shape=jax.ShapeDtypeStruct(total.shape, bf16),
        in_specs=[pl.BlockSpec(memory_space=pltpu.SMEM)] + [vmem] * (XN + 2),
        out_specs=vmem,
        compiler_params=pltpu.CompilerParams(vmem_limit_bytes=SMALL_VMEM),
        cost_estimate=pl.CostEstimate(
            flops=2 * SEC * (XN - 1) * WH * 768, bytes_accessed=3_000_000, transcendentals=0
        ),
        name="finish",
    )(place, *pieces, w_out, total, gate)


def seq_send(array, target_of):
    pairs = []
    for z in range(ZN):
        for y in range(YN):
            for c in range(CN):
                tz, ty, tc = target_of(z, y, c)
                target = (tz % ZN * YN + ty % YN) * CN + tc % CN
                pairs.append(((z * YN + y) * CN + c, target))
    return lax.ppermute(array, "seq", pairs)


def ring(array):
    return seq_send(array, lambda z, y, c: (z + 1 - 2 * c, y, c))


def swap(array):
    return seq_send(array, lambda z, y, c: (z, y, c + 1))


def after(array, others):
    return lax.optimization_barrier((array, others))[0]


def y_shift(array, dy):
    return seq_send(array, lambda z, y, c: (z, y + dy, c))


def tp_shift(array, dx):
    return lax.ppermute(array, "tp", [(x, (x + dx) % XN) for x in range(XN)])


def local(section, history, levels, mlp_cached, w_qkv, w_out, modulation, level_embed):
    key_value, query = prep(section, history, levels, w_qkv, modulation, level_embed)
    first, second = [key_value], [swap(key_value)]
    first.append(ring(first[0]))
    second.append(ring(second[0]))
    queries = [y_shift(query, dy) for dy in (1, 2, 3)]
    query, first[0] = stage(query, key_value)
    first[1] = after(first[1], queries[:2])
    first.append(ring(first[1]))
    second[1] = after(second[1], (queries, query, first[0]))
    second.append(ring(second[1]))
    first.append(ring(first[2]))
    queries = [query] + queries
    state = attend(queries, [first[0], second[0], first[1], second[1]], None, False)
    others = [swap(after(chunk, state)) for chunk in (first[1], second[1])]
    second[2] = after(second[2], state)
    second.append(ring(second[2]))
    first[3] = after(first[3], state)
    first.append(ring(first[3]))
    others_2 = [swap(chunk) for chunk in (after(first[2], state), second[2])]
    state = attend(queries, others + [first[2], second[2]], state, False)
    others_3 = [swap(after(chunk, state)) for chunk in (first[3], second[3])]
    state = attend(queries, others_2 + [first[3], second[3]], state, False)
    first[4] = after(first[4], state)
    state = attend(queries, others_3, state, False)
    parts = attend(queries, [first[4], swap(first[4])], state, True)
    sent = [y_shift(parts[dy], -dy) for dy in (2, 1, 3)]
    attended = merge([parts[0]] + sent)
    place = lax.axis_index("tp").astype(jnp.int32).reshape(1)
    pieces = [tp_shift(attended, dx) for dx in (2, 1, 3)]
    total, gate = begin(place, attended, w_out, section, modulation, mlp_cached)
    return finish(place, pieces, w_out, total, gate)


def solution(mesh):
    return jax.shard_map(
        local,
        mesh=mesh,
        in_specs=(
            P("seq", None),
            P("seq", None),
            P("seq"),
            P("seq", "tp"),
            P(None, None, "tp"),
            P(None, "tp"),
            P(),
            P(),
        ),
        out_specs=P("seq", "tp"),
        check_vma=False,
    )
```

```python
import functools
import math

import jax
import jax.numpy as jnp
from jax import lax
from jax.experimental import pallas as pl
from jax.experimental.pallas import tpu as pltpu
from jax.sharding import PartitionSpec as P

HD = 128
HEADS_DEV = 3
WH = HEADS_DEV * HD
D = 3072
ZN, YN, CN, XN = 8, 4, 2, 4
SEC = 128
CTX = 64
ROWS = SEC + CTX
FT = 64
FRAMES = 4
STAT_ROWS = 16
PAD_KEY = 2.0**126
PAD_TEST = 2.0**125
TO_LOG2 = HD**-0.5 * math.log2(math.e)
MIB = 1024 * 1024
PREP_VMEM = 63 * MIB
ATTEND_VMEM = 24 * MIB
SMALL_VMEM = 8 * MIB

f32 = jnp.float32
bf16 = jnp.bfloat16


def norm_rows(rows, shift_row, scale_row):
    row_mean = jnp.mean(rows, axis=-1, keepdims=True)
    centred = rows - row_mean
    spread = jnp.mean(centred * centred, axis=-1, keepdims=True)
    return (centred * lax.rsqrt(spread + 1e-06) * (1.0 + scale_row) + shift_row).astype(bf16)


def prep_kernel(
    levels_in, modulation_in, embed_in, section, history, w_qkv,
    key_value, queries,
    levels, modulation, level_embed, sec_buf, hist_buf, w_buf, pooled, rows_h, sems,
):
    half = D // 2
    spans = [pl.ds(0, half), pl.ds(half, half)]
    copies = [
        pltpu.make_async_copy(levels_in, levels, sems.at[0]),
        pltpu.make_async_copy(modulation_in, modulation, sems.at[1]),
        pltpu.make_async_copy(section, sec_buf, sems.at[2]),
        pltpu.make_async_copy(history, hist_buf, sems.at[3]),
        pltpu.make_async_copy(embed_in, level_embed, sems.at[4]),
    ]
    weight_copies = [
        pltpu.make_async_copy(
            w_qkv.at[which, spans[part]],
            w_buf.at[spans[part], pl.ds(place * WH, WH)],
            sems.at[5 + index],
        )
        for index, (which, place, part) in enumerate(
            ((0, 2, 0), (0, 2, 1), (1, 0, 0), (2, 1, 0), (1, 0, 1), (2, 1, 1))
        )
    ]
    for copy in copies[:3] + weight_copies[:2] + copies[3:] + weight_copies[2:]:
        copy.start()

    copies[1].wait()
    shift_row = modulation[0:1, :]
    scale_row = modulation[1:2, :]
    copies[2].wait()

    def section_step(step, carry):
        span = pl.ds(pl.multiple_of(step * 16, 16), 16)
        rows_h[span, :] = norm_rows(sec_buf[span, :].astype(f32), shift_row, scale_row)
        return carry

    lax.fori_loop(0, SEC // 16, section_step, 0, unroll=4)

    copies[0].wait()
    counts = []
    starts = []
    total = jnp.int32(0)
    for frame in range(FRAMES):
        starts.append(total)
        counts.append(lax.shift_right_logical(jnp.int32(FT // 2), levels[frame]))
        total = total + counts[frame]

    slot = lax.broadcasted_iota(jnp.int32, (CTX, FRAMES * FT), 0)
    source = lax.broadcasted_iota(jnp.int32, (CTX, FRAMES * FT), 1)
    factors = jnp.zeros((CTX, FRAMES * FT), f32)
    for frame in range(FRAMES):
        width = lax.shift_left(jnp.int32(2), levels[frame])
        first = (slot - starts[frame]) * width + frame * FT
        inside = (
            (source >= first)
            & (source < first + width)
            & (source >= frame * FT)
            & (source < (frame + 1) * FT)
        )
        factors = factors + jnp.where(inside, 1.0 / width.astype(f32), 0.0)
    copies[3].wait()
    pooled[...] = jnp.dot(factors.astype(bf16), hist_buf[...], preferred_element_type=f32)
    copies[4].wait()

    weight_copies[0].wait()
    weight_copies[1].wait()
    asked = jnp.dot(rows_h[:SEC, :], w_buf[:, 2 * WH :], preferred_element_type=f32)
    for step in range(CTX // 16):
        span = slice(step * 16, (step + 1) * 16)
        rows = pooled[span, :]
        index = lax.broadcasted_iota(jnp.int32, (16, 1), 0) + step * 16
        for frame in range(FRAMES):
            mine = (index >= starts[frame]) & (index < starts[frame] + counts[frame])
            rows = rows + jnp.where(mine, level_embed[pl.ds(levels[frame], 1), :], 0.0)
        rows_h[SEC + step * 16 : SEC + (step + 1) * 16, :] = norm_rows(
            rows, shift_row, scale_row
        )
    queries[...] = (asked * TO_LOG2).astype(bf16)

    both = None
    for part in range(2):
        weight_copies[2 + 2 * part].wait()
        weight_copies[3 + 2 * part].wait()
        span = slice(part * half, (part + 1) * half)
        piece = jnp.dot(
            rows_h[:, span], w_buf[span, : 2 * WH], preferred_element_type=f32
        )
        both = piece if part == 0 else both + piece
    row_index = lax.broadcasted_iota(jnp.int32, (ROWS, WH), 0)
    key_value[0] = jnp.where(row_index < SEC + total, both[:, :WH], PAD_KEY).astype(bf16)
    key_value[1] = both[:, WH:].astype(bf16)


def prep(section, history, levels, w_qkv, modulation, level_embed):
    any_spec = pl.BlockSpec(memory_space=pl.ANY)
    vmem = pl.BlockSpec(memory_space=pltpu.VMEM)
    return pl.pallas_call(
        prep_kernel,
        out_shape=(
            jax.ShapeDtypeStruct((2, ROWS, WH), bf16),
            jax.ShapeDtypeStruct((SEC, WH), bf16),
        ),
        in_specs=[any_spec] * 6,
        out_specs=(vmem, vmem),
        scratch_shapes=[
            pltpu.SMEM((FRAMES,), jnp.int32),
            pltpu.VMEM((3, D), f32),
            pltpu.VMEM((4, D), f32),
            pltpu.VMEM((SEC, D), bf16),
            pltpu.VMEM((FRAMES * FT, D), bf16),
            pltpu.VMEM((D, 3 * WH), bf16),
            pltpu.VMEM((CTX, D), f32),
            pltpu.VMEM((ROWS, D), bf16),
            pltpu.SemaphoreType.DMA((11,)),
        ],
        compiler_params=pltpu.CompilerParams(vmem_limit_bytes=PREP_VMEM),
        cost_estimate=pl.CostEstimate(
            flops=2 * ROWS * D * 3 * WH, bytes_accessed=12_000_000, transcendentals=0
        ),
        name="prep",
    )(levels, modulation, level_embed, section, history, w_qkv)


def stage_kernel(query_in, block_in, query, block, sems):
    copies = [
        pltpu.make_async_copy(query_in, query, sems.at[0]),
        pltpu.make_async_copy(block_in, block, sems.at[1]),
    ]
    for copy in copies:
        copy.start()
    for copy in copies:
        copy.wait()


def stage(query, block):
    any_spec = pl.BlockSpec(memory_space=pl.ANY)
    vmem = pl.BlockSpec(memory_space=pltpu.VMEM)
    return pl.pallas_call(
        stage_kernel,
        out_shape=(
            jax.ShapeDtypeStruct(query.shape, bf16),
            jax.ShapeDtypeStruct(block.shape, bf16),
        ),
        in_specs=[any_spec, any_spec],
        out_specs=(vmem, vmem),
        scratch_shapes=[pltpu.SemaphoreType.DMA((2,))],
        compiler_params=pltpu.CompilerParams(vmem_limit_bytes=SMALL_VMEM),
        cost_estimate=pl.CostEstimate(flops=0, bytes_accessed=800_000, transcendentals=0),
        name="stage",
    )(query, block)


def attend_kernel(block_shapes, first, last, *refs):
    refs = list(refs)
    query_refs = [refs.pop(0) for _ in range(YN)]
    blocks = []
    for joint in block_shapes:
        if joint:
            ref = refs.pop(0)
            blocks.append((ref.at[0], ref.at[1]))
        else:
            key_ref = refs.pop(0)
            blocks.append((key_ref, refs.pop(0)))
    if not first:
        max_in, den_in, num_in = refs.pop(0), refs.pop(0), refs.pop(0)
    outs = refs
    pad = [key_ref[SEC:ROWS, 0:1].astype(f32) > PAD_TEST for key_ref, _ in blocks]

    def all_scores(head, pair):
        cols = slice(head * HD, (head + 1) * HD)
        query = jnp.concatenate(
            [query_refs[2 * pair][:, cols], query_refs[2 * pair + 1][:, cols]], axis=0
        )
        scores = []
        for (key_ref, _), pad_rows in zip(blocks, pad):
            score = lax.dot_general(
                key_ref[:, cols], query, (((1,), (1,)), ((), ())), preferred_element_type=f32
            )
            scores.append(score[:SEC])
            scores.append(jnp.where(pad_rows, -1e30, score[SEC:]))
        return scores

    order = [(head, pair) for head in range(HEADS_DEV) for pair in range(YN // 2)]
    coming = all_scores(*order[0])
    for place, (head, pair) in enumerate(order):
        cols = slice(head * HD, (head + 1) * HD)
        lanes = slice(pair * 2 * SEC, (pair + 1) * 2 * SEC)
        scores = coming
        if place + 1 < len(order):
            coming = all_scores(*order[place + 1])
        if True:
            new_max = functools.reduce(
                jnp.maximum, [jnp.max(score, axis=0, keepdims=True) for score in scores]
            )
            if not first:
                old_max = max_in[head : head + 1, lanes]
                new_max = jnp.maximum(new_max, old_max)
                rescale = jnp.exp2(old_max - new_max)
                denominator = den_in[head : head + 1, lanes] * rescale
                numerator = num_in[cols, lanes] * rescale
            else:
                denominator = jnp.zeros((1, 2 * SEC), f32)
                numerator = jnp.zeros((HD, 2 * SEC), f32)
            for index, (_, value_ref) in enumerate(blocks):
                expon = [
                    jnp.exp2(score - new_max) for score in scores[2 * index : 2 * index + 2]
                ]
                for part in expon:
                    denominator = denominator + jnp.sum(part, axis=0, keepdims=True)
                weights = jnp.concatenate([part.astype(bf16) for part in expon], axis=0)
                numerator = numerator + lax.dot_general(
                    value_ref[:, cols], weights, (((0,), (0,)), ((), ())),
                    preferred_element_type=f32,
                )
            if not last:
                outs[0][head : head + 1, lanes] = new_max
                outs[1][head : head + 1, lanes] = denominator
                outs[2][cols, lanes] = numerator
            else:
                local_out = (numerator / denominator).astype(bf16)
                stat = new_max + jnp.log2(denominator)
                high = stat.astype(bf16).astype(f32)
                middle = (stat - high).astype(bf16).astype(f32)
                low = stat - high - middle
                for half in range(2):
                    piece = slice(half * SEC, (half + 1) * SEC)
                    out = outs[2 * pair + half]
                    out[cols, :] = local_out[:, piece]
                    block = jnp.concatenate(
                        [high[:, piece], middle[:, piece], low[:, piece]], axis=0
                    )
                    stats_ref = outs[YN + 2 * pair + half]
                    stats_ref[head * 3 : head * 3 + 3, :] = block
    if last:
        for index in range(YN):
            stats_ref = outs[YN + index]
            stats_ref[3 * HEADS_DEV : STAT_ROWS, :] = jnp.zeros(
                (STAT_ROWS - 3 * HEADS_DEV, SEC), f32
            )
            outs[index][WH : WH + STAT_ROWS, :] = stats_ref[...].astype(bf16)


def attend(queries, blocks, state, last):
    vmem = pl.BlockSpec(memory_space=pltpu.VMEM)
    block_shapes = tuple(not isinstance(block, tuple) for block in blocks)
    flat = []
    for block in blocks:
        flat.extend(block if isinstance(block, tuple) else (block,))
    operands = list(queries) + flat + (list(state) if state is not None else [])
    count = len(blocks)
    if last:
        out_shape = tuple(
            jax.ShapeDtypeStruct((WH + STAT_ROWS, SEC), bf16) for _ in range(YN)
        )
        scratch = [pltpu.VMEM((STAT_ROWS, SEC), f32) for _ in range(YN)]
    else:
        out_shape = (
            jax.ShapeDtypeStruct((HEADS_DEV, YN * SEC), f32),
            jax.ShapeDtypeStruct((HEADS_DEV, YN * SEC), f32),
            jax.ShapeDtypeStruct((WH, YN * SEC), f32),
        )
        scratch = []
    return pl.pallas_call(
        functools.partial(attend_kernel, block_shapes, state is None, last),
        out_shape=out_shape,
        in_specs=[vmem] * len(operands),
        out_specs=tuple([vmem] * len(out_shape)),
        scratch_shapes=scratch,
        compiler_params=pltpu.CompilerParams(vmem_limit_bytes=ATTEND_VMEM),
        cost_estimate=pl.CostEstimate(
            flops=4 * count * ROWS * YN * SEC * WH,
            bytes_accessed=count * ROWS * WH * 4 + 2_000_000,
            transcendentals=count * ROWS * YN * SEC * HEADS_DEV,
        ),
        name="attend",
    )(*operands)


def merge_kernel(*refs):
    parts, out = refs[:YN], refs[YN]
    for head in range(HEADS_DEV):
        cols = slice(head * HD, (head + 1) * HD)
        stats = []
        for part in parts:
            block = part[WH : WH + STAT_ROWS, :].astype(f32)
            stats.append(
                block[3 * head : 3 * head + 1]
                + block[3 * head + 1 : 3 * head + 2]
                + block[3 * head + 2 : 3 * head + 3]
            )
        top = functools.reduce(jnp.maximum, stats)
        shares = [jnp.exp2(stat - top) for stat in stats]
        whole = functools.reduce(jnp.add, shares)
        total = functools.reduce(
            jnp.add, [part[cols, :].astype(f32) * share for part, share in zip(parts, shares)]
        )
        out[:, cols] = jnp.transpose(total / whole).astype(bf16)


def merge(parts):
    vmem = pl.BlockSpec(memory_space=pltpu.VMEM)
    return pl.pallas_call(
        merge_kernel,
        out_shape=jax.ShapeDtypeStruct((SEC, WH), bf16),
        in_specs=[vmem] * YN,
        out_specs=vmem,
        compiler_params=pltpu.CompilerParams(vmem_limit_bytes=SMALL_VMEM),
        cost_estimate=pl.CostEstimate(flops=500_000, bytes_accessed=500_000, transcendentals=0),
        name="merge",
    )(*parts)


def owned_rows(w_out, owner):
    return w_out[pl.ds(pl.multiple_of(owner * WH, WH), WH), :]


def begin_kernel(place, piece, w_out, section, modulation, mlp, total, gate):
    me = place[0]
    width = total.shape[1]
    cols = pl.ds(pl.multiple_of(me * width, width), width)
    gate[...] = modulation[2:3, cols]
    product = jnp.dot(piece[...], owned_rows(w_out, me), preferred_element_type=f32)
    total[...] = section[:, cols].astype(f32) + gate[...] * (product + mlp[...].astype(f32))


def begin(place, piece, w_out, section, modulation, mlp_cached):
    vmem = pl.BlockSpec(memory_space=pltpu.VMEM)
    return pl.pallas_call(
        begin_kernel,
        out_shape=(
            jax.ShapeDtypeStruct(mlp_cached.shape, f32),
            jax.ShapeDtypeStruct((1, mlp_cached.shape[1]), f32),
        ),
        in_specs=[pl.BlockSpec(memory_space=pltpu.SMEM)] + [vmem] * 5,
        out_specs=(vmem, vmem),
        compiler_params=pltpu.CompilerParams(vmem_limit_bytes=SMALL_VMEM),
        cost_estimate=pl.CostEstimate(
            flops=2 * SEC * WH * 768, bytes_accessed=4_000_000, transcendentals=0
        ),
        name="begin",
    )(place, piece, w_out, section, modulation, mlp_cached)


def add_kernel(shift, place, piece, w_out, base, gate, out):
    rows = owned_rows(w_out, lax.rem(place[0] - shift + XN, XN))
    product = jnp.dot(piece[...], rows, preferred_element_type=f32)
    out[...] = (base[...] + gate[...] * product).astype(out.dtype)


def add_piece(shift, dtype, place, piece, w_out, total, gate):
    vmem = pl.BlockSpec(memory_space=pltpu.VMEM)
    return pl.pallas_call(
        functools.partial(add_kernel, shift),
        out_shape=jax.ShapeDtypeStruct(total.shape, dtype),
        in_specs=[pl.BlockSpec(memory_space=pltpu.SMEM)] + [vmem] * 4,
        out_specs=vmem,
        compiler_params=pltpu.CompilerParams(vmem_limit_bytes=SMALL_VMEM),
        cost_estimate=pl.CostEstimate(
            flops=2 * SEC * WH * 768, bytes_accessed=1_000_000, transcendentals=0
        ),
        name="add_piece",
    )(place, piece, w_out, total, gate)


def seq_send(array, target_of):
    pairs = []
    for z in range(ZN):
        for y in range(YN):
            for c in range(CN):
                tz, ty, tc = target_of(z, y, c)
                target = (tz % ZN * YN + ty % YN) * CN + tc % CN
                pairs.append(((z * YN + y) * CN + c, target))
    return lax.ppermute(array, "seq", pairs)


def ring(array):
    return seq_send(array, lambda z, y, c: (z + 1 - 2 * c, y, c))


def swap(array):
    return seq_send(array, lambda z, y, c: (z, y, c + 1))


def after(array, others):
    return lax.optimization_barrier((array, others))[0]


def y_shift(array, dy):
    return seq_send(array, lambda z, y, c: (z, y + dy, c))


def tp_shift(array, dx):
    return lax.ppermute(array, "tp", [(x, (x + dx) % XN) for x in range(XN)])


def local(section, history, levels, mlp_cached, w_qkv, w_out, modulation, level_embed):
    key_value, query = prep(section, history, levels, w_qkv, modulation, level_embed)
    first, second = [key_value], [swap(key_value)]
    first.append(ring(first[0]))
    second.append(ring(second[0]))
    queries = [y_shift(after(query, second[0]), 1)] + [y_shift(query, dy) for dy in (2, 3)]
    query, first[0] = stage(query, key_value)
    first[1] = after(first[1], (queries[:2], query, first[0]))
    first.append(ring(first[1]))
    second.append(ring(second[1]))
    first[2] = after(first[2], queries[2])
    first.append(ring(first[2]))
    queries = [query] + queries
    state = attend(queries, [first[0], second[0], first[1], second[1]], None, False)
    others = [swap(chunk) for chunk in (first[1], second[1])]
    second[2] = after(second[2], state)
    second.append(ring(second[2]))
    first[3] = after(first[3], state)
    first.append(ring(first[3]))
    others_2 = [swap(chunk) for chunk in (after(first[2], state), second[2])]
    state = attend(queries, others + [first[2], second[2]], state, False)
    others = [swap(after(chunk, state)) for chunk in (first[3], second[3])]
    state = attend(queries, others_2 + [first[3], second[3]], state, False)
    first[4] = after(first[4], state)
    state = attend(queries, others, state, False)
    parts = attend(queries, [first[4], swap(first[4])], state, True)
    sent = [y_shift(parts[dy], -dy) for dy in (2, 1, 3)]
    attended = merge([parts[0]] + sent)
    place = lax.axis_index("tp").astype(jnp.int32).reshape(1)
    pieces = {dx: tp_shift(attended, dx) for dx in (3, 1, 2)}
    total, gate = begin(place, attended, w_out, section, modulation, mlp_cached)
    for dx, dtype in ((3, f32), (1, f32), (2, bf16)):
        total = add_piece(dx, dtype, place, pieces[dx], w_out, total, gate)
    return total


def solution(mesh):
    return jax.shard_map(
        local,
        mesh=mesh,
        in_specs=(
            P("seq", None),
            P("seq", None),
            P("seq"),
            P("seq", "tp"),
            P(None, None, "tp"),
            P(None, "tp"),
            P(),
            P(),
        ),
        out_specs=P("seq", "tp"),
        check_vma=False,
    )
```

```python
import functools
import math

import jax
import jax.numpy as jnp
from jax import lax
from jax.experimental import pallas as pl
from jax.experimental.pallas import tpu as pltpu
from jax.sharding import PartitionSpec as P

HD = 128
HEADS_DEV = 3
WH = HEADS_DEV * HD
D = 3072
ZN, YN, CN, XN = 8, 4, 2, 4
SEC = 128
CTX = 64
ROWS = SEC + CTX
FT = 64
FRAMES = 4
STAT_ROWS = 16
PAD_KEY = 2.0**126
PAD_TEST = 2.0**125
TO_LOG2 = HD**-0.5 * math.log2(math.e)
MIB = 1024 * 1024
PREP_VMEM = 63 * MIB
ATTEND_VMEM = 24 * MIB
SMALL_VMEM = 8 * MIB

f32 = jnp.float32
bf16 = jnp.bfloat16


def norm_rows(rows, shift_row, scale_row):
    row_mean = jnp.mean(rows, axis=-1, keepdims=True)
    centred = rows - row_mean
    spread = jnp.mean(centred * centred, axis=-1, keepdims=True)
    return (centred * lax.rsqrt(spread + 1e-06) * (1.0 + scale_row) + shift_row).astype(bf16)


def prep_kernel(
    levels_in, modulation_in, embed_in, section, history, w_qkv,
    key_value, queries,
    levels, modulation, level_embed, sec_buf, hist_buf, w_buf, pooled, rows_h, sems,
):
    half = D // 2
    spans = [pl.ds(0, half), pl.ds(half, half)]
    copies = [
        pltpu.make_async_copy(levels_in, levels, sems.at[0]),
        pltpu.make_async_copy(modulation_in, modulation, sems.at[1]),
        pltpu.make_async_copy(section, sec_buf, sems.at[2]),
        pltpu.make_async_copy(history, hist_buf, sems.at[3]),
        pltpu.make_async_copy(embed_in, level_embed, sems.at[4]),
    ]
    weight_copies = [
        pltpu.make_async_copy(
            w_qkv.at[which, spans[part]],
            w_buf.at[spans[part], pl.ds(place * WH, WH)],
            sems.at[5 + index],
        )
        for index, (which, place, part) in enumerate(
            ((0, 2, 0), (0, 2, 1), (1, 0, 0), (2, 1, 0), (1, 0, 1), (2, 1, 1))
        )
    ]
    for copy in copies[:3] + weight_copies[:2] + copies[3:] + weight_copies[2:]:
        copy.start()

    copies[1].wait()
    shift_row = modulation[0:1, :]
    scale_row = modulation[1:2, :]
    copies[2].wait()

    def section_step(step, carry):
        span = pl.ds(pl.multiple_of(step * 16, 16), 16)
        rows_h[span, :] = norm_rows(sec_buf[span, :].astype(f32), shift_row, scale_row)
        return carry

    lax.fori_loop(0, SEC // 16, section_step, 0, unroll=4)

    copies[0].wait()
    counts = []
    starts = []
    total = jnp.int32(0)
    for frame in range(FRAMES):
        starts.append(total)
        counts.append(lax.shift_right_logical(jnp.int32(FT // 2), levels[frame]))
        total = total + counts[frame]

    slot = lax.broadcasted_iota(jnp.int32, (CTX, FRAMES * FT), 0)
    source = lax.broadcasted_iota(jnp.int32, (CTX, FRAMES * FT), 1)
    factors = jnp.zeros((CTX, FRAMES * FT), f32)
    for frame in range(FRAMES):
        width = lax.shift_left(jnp.int32(2), levels[frame])
        first = (slot - starts[frame]) * width + frame * FT
        inside = (
            (source >= first)
            & (source < first + width)
            & (source >= frame * FT)
            & (source < (frame + 1) * FT)
        )
        factors = factors + jnp.where(inside, 1.0 / width.astype(f32), 0.0)
    copies[3].wait()
    pooled[...] = jnp.dot(factors.astype(bf16), hist_buf[...], preferred_element_type=f32)
    copies[4].wait()

    weight_copies[0].wait()
    weight_copies[1].wait()
    asked = jnp.dot(rows_h[:SEC, :], w_buf[:, 2 * WH :], preferred_element_type=f32)
    for step in range(CTX // 16):
        span = slice(step * 16, (step + 1) * 16)
        rows = pooled[span, :]
        index = lax.broadcasted_iota(jnp.int32, (16, 1), 0) + step * 16
        for frame in range(FRAMES):
            mine = (index >= starts[frame]) & (index < starts[frame] + counts[frame])
            rows = rows + jnp.where(mine, level_embed[pl.ds(levels[frame], 1), :], 0.0)
        rows_h[SEC + step * 16 : SEC + (step + 1) * 16, :] = norm_rows(
            rows, shift_row, scale_row
        )
    queries[...] = (asked * TO_LOG2).astype(bf16)

    both = None
    for part in range(2):
        weight_copies[2 + 2 * part].wait()
        weight_copies[3 + 2 * part].wait()
        span = slice(part * half, (part + 1) * half)
        piece = jnp.dot(
            rows_h[:, span], w_buf[span, : 2 * WH], preferred_element_type=f32
        )
        both = piece if part == 0 else both + piece
    row_index = lax.broadcasted_iota(jnp.int32, (ROWS, WH), 0)
    key_value[0] = jnp.where(row_index < SEC + total, both[:, :WH], PAD_KEY).astype(bf16)
    key_value[1] = both[:, WH:].astype(bf16)


def prep(section, history, levels, w_qkv, modulation, level_embed):
    any_spec = pl.BlockSpec(memory_space=pl.ANY)
    vmem = pl.BlockSpec(memory_space=pltpu.VMEM)
    return pl.pallas_call(
        prep_kernel,
        out_shape=(
            jax.ShapeDtypeStruct((2, ROWS, WH), bf16),
            jax.ShapeDtypeStruct((SEC, WH), bf16),
        ),
        in_specs=[any_spec] * 6,
        out_specs=(vmem, vmem),
        scratch_shapes=[
            pltpu.SMEM((FRAMES,), jnp.int32),
            pltpu.VMEM((3, D), f32),
            pltpu.VMEM((4, D), f32),
            pltpu.VMEM((SEC, D), bf16),
            pltpu.VMEM((FRAMES * FT, D), bf16),
            pltpu.VMEM((D, 3 * WH), bf16),
            pltpu.VMEM((CTX, D), f32),
            pltpu.VMEM((ROWS, D), bf16),
            pltpu.SemaphoreType.DMA((11,)),
        ],
        compiler_params=pltpu.CompilerParams(vmem_limit_bytes=PREP_VMEM),
        cost_estimate=pl.CostEstimate(
            flops=2 * ROWS * D * 3 * WH, bytes_accessed=12_000_000, transcendentals=0
        ),
        name="prep",
    )(levels, modulation, level_embed, section, history, w_qkv)


def stage_kernel(query_in, block_in, query, block, sems):
    copies = [
        pltpu.make_async_copy(query_in, query, sems.at[0]),
        pltpu.make_async_copy(block_in, block, sems.at[1]),
    ]
    for copy in copies:
        copy.start()
    for copy in copies:
        copy.wait()


def stage(query, block):
    any_spec = pl.BlockSpec(memory_space=pl.ANY)
    vmem = pl.BlockSpec(memory_space=pltpu.VMEM)
    return pl.pallas_call(
        stage_kernel,
        out_shape=(
            jax.ShapeDtypeStruct(query.shape, bf16),
            jax.ShapeDtypeStruct(block.shape, bf16),
        ),
        in_specs=[any_spec, any_spec],
        out_specs=(vmem, vmem),
        scratch_shapes=[pltpu.SemaphoreType.DMA((2,))],
        compiler_params=pltpu.CompilerParams(vmem_limit_bytes=SMALL_VMEM),
        cost_estimate=pl.CostEstimate(flops=0, bytes_accessed=800_000, transcendentals=0),
        name="stage",
    )(query, block)


def attend_kernel(block_shapes, first, last, *refs):
    refs = list(refs)
    query_refs = [refs.pop(0) for _ in range(YN)]
    blocks = []
    for joint in block_shapes:
        if joint:
            ref = refs.pop(0)
            blocks.append((ref.at[0], ref.at[1]))
        else:
            key_ref = refs.pop(0)
            blocks.append((key_ref, refs.pop(0)))
    if not first:
        max_in, den_in, num_in = refs.pop(0), refs.pop(0), refs.pop(0)
    outs = refs
    pad = [key_ref[SEC:ROWS, 0:1].astype(f32) > PAD_TEST for key_ref, _ in blocks]

    def all_scores(head, pair):
        cols = slice(head * HD, (head + 1) * HD)
        query = jnp.concatenate(
            [query_refs[2 * pair][:, cols], query_refs[2 * pair + 1][:, cols]], axis=0
        )
        scores = []
        for (key_ref, _), pad_rows in zip(blocks, pad):
            score = lax.dot_general(
                key_ref[:, cols], query, (((1,), (1,)), ((), ())), preferred_element_type=f32
            )
            scores.append(score[:SEC])
            scores.append(jnp.where(pad_rows, -1e30, score[SEC:]))
        return scores

    order = [(head, pair) for head in range(HEADS_DEV) for pair in range(YN // 2)]
    coming = all_scores(*order[0])
    for place, (head, pair) in enumerate(order):
        cols = slice(head * HD, (head + 1) * HD)
        lanes = slice(pair * 2 * SEC, (pair + 1) * 2 * SEC)
        scores = coming
        if place + 1 < len(order):
            coming = all_scores(*order[place + 1])
        if True:
            new_max = functools.reduce(
                jnp.maximum, [jnp.max(score, axis=0, keepdims=True) for score in scores]
            )
            if not first:
                old_max = max_in[head : head + 1, lanes]
                new_max = jnp.maximum(new_max, old_max)
                rescale = jnp.exp2(old_max - new_max)
                denominator = den_in[head : head + 1, lanes] * rescale
                numerator = num_in[cols, lanes] * rescale
            else:
                denominator = jnp.zeros((1, 2 * SEC), f32)
                numerator = jnp.zeros((HD, 2 * SEC), f32)
            for index, (_, value_ref) in enumerate(blocks):
                expon = [
                    jnp.exp2(score - new_max) for score in scores[2 * index : 2 * index + 2]
                ]
                for part in expon:
                    denominator = denominator + jnp.sum(part, axis=0, keepdims=True)
                weights = jnp.concatenate([part.astype(bf16) for part in expon], axis=0)
                numerator = numerator + lax.dot_general(
                    value_ref[:, cols], weights, (((0,), (0,)), ((), ())),
                    preferred_element_type=f32,
                )
            if not last:
                outs[0][head : head + 1, lanes] = new_max
                outs[1][head : head + 1, lanes] = denominator
                outs[2][cols, lanes] = numerator
            else:
                local_out = (numerator / denominator).astype(bf16)
                stat = new_max + jnp.log2(denominator)
                high = stat.astype(bf16).astype(f32)
                middle = (stat - high).astype(bf16).astype(f32)
                low = stat - high - middle
                for half in range(2):
                    piece = slice(half * SEC, (half + 1) * SEC)
                    out = outs[2 * pair + half]
                    out[cols, :] = local_out[:, piece]
                    block = jnp.concatenate(
                        [high[:, piece], middle[:, piece], low[:, piece]], axis=0
                    )
                    stats_ref = outs[YN + 2 * pair + half]
                    stats_ref[head * 3 : head * 3 + 3, :] = block
    if last:
        for index in range(YN):
            stats_ref = outs[YN + index]
            stats_ref[3 * HEADS_DEV : STAT_ROWS, :] = jnp.zeros(
                (STAT_ROWS - 3 * HEADS_DEV, SEC), f32
            )
            outs[index][WH : WH + STAT_ROWS, :] = stats_ref[...].astype(bf16)


def attend(queries, blocks, state, last):
    vmem = pl.BlockSpec(memory_space=pltpu.VMEM)
    block_shapes = tuple(not isinstance(block, tuple) for block in blocks)
    flat = []
    for block in blocks:
        flat.extend(block if isinstance(block, tuple) else (block,))
    operands = list(queries) + flat + (list(state) if state is not None else [])
    count = len(blocks)
    if last:
        out_shape = tuple(
            jax.ShapeDtypeStruct((WH + STAT_ROWS, SEC), bf16) for _ in range(YN)
        )
        scratch = [pltpu.VMEM((STAT_ROWS, SEC), f32) for _ in range(YN)]
    else:
        out_shape = (
            jax.ShapeDtypeStruct((HEADS_DEV, YN * SEC), f32),
            jax.ShapeDtypeStruct((HEADS_DEV, YN * SEC), f32),
            jax.ShapeDtypeStruct((WH, YN * SEC), f32),
        )
        scratch = []
    return pl.pallas_call(
        functools.partial(attend_kernel, block_shapes, state is None, last),
        out_shape=out_shape,
        in_specs=[vmem] * len(operands),
        out_specs=tuple([vmem] * len(out_shape)),
        scratch_shapes=scratch,
        compiler_params=pltpu.CompilerParams(vmem_limit_bytes=ATTEND_VMEM),
        cost_estimate=pl.CostEstimate(
            flops=4 * count * ROWS * YN * SEC * WH,
            bytes_accessed=count * ROWS * WH * 4 + 2_000_000,
            transcendentals=count * ROWS * YN * SEC * HEADS_DEV,
        ),
        name="attend",
    )(*operands)


def merge_kernel(*refs):
    parts, out = refs[:YN], refs[YN]
    for head in range(HEADS_DEV):
        cols = slice(head * HD, (head + 1) * HD)
        stats = []
        for part in parts:
            block = part[WH : WH + STAT_ROWS, :].astype(f32)
            stats.append(
                block[3 * head : 3 * head + 1]
                + block[3 * head + 1 : 3 * head + 2]
                + block[3 * head + 2 : 3 * head + 3]
            )
        top = functools.reduce(jnp.maximum, stats)
        shares = [jnp.exp2(stat - top) for stat in stats]
        whole = functools.reduce(jnp.add, shares)
        total = functools.reduce(
            jnp.add, [part[cols, :].astype(f32) * share for part, share in zip(parts, shares)]
        )
        out[:, cols] = jnp.transpose(total / whole).astype(bf16)


def merge(parts):
    vmem = pl.BlockSpec(memory_space=pltpu.VMEM)
    return pl.pallas_call(
        merge_kernel,
        out_shape=jax.ShapeDtypeStruct((SEC, WH), bf16),
        in_specs=[vmem] * YN,
        out_specs=vmem,
        compiler_params=pltpu.CompilerParams(vmem_limit_bytes=SMALL_VMEM),
        cost_estimate=pl.CostEstimate(flops=500_000, bytes_accessed=500_000, transcendentals=0),
        name="merge",
    )(*parts)


def owned_rows(w_out, owner):
    return w_out[pl.ds(pl.multiple_of(owner * WH, WH), WH), :]


def begin_kernel(place, piece, w_out, section, modulation, mlp, total, gate):
    me = place[0]
    width = total.shape[1]
    cols = pl.ds(pl.multiple_of(me * width, width), width)
    gate[...] = modulation[2:3, cols]
    product = jnp.dot(piece[...], owned_rows(w_out, me), preferred_element_type=f32)
    total[...] = section[:, cols].astype(f32) + gate[...] * (product + mlp[...].astype(f32))


def begin(place, piece, w_out, section, modulation, mlp_cached):
    vmem = pl.BlockSpec(memory_space=pltpu.VMEM)
    return pl.pallas_call(
        begin_kernel,
        out_shape=(
            jax.ShapeDtypeStruct(mlp_cached.shape, f32),
            jax.ShapeDtypeStruct((1, mlp_cached.shape[1]), f32),
        ),
        in_specs=[pl.BlockSpec(memory_space=pltpu.SMEM)] + [vmem] * 5,
        out_specs=(vmem, vmem),
        compiler_params=pltpu.CompilerParams(vmem_limit_bytes=SMALL_VMEM),
        cost_estimate=pl.CostEstimate(
            flops=2 * SEC * WH * 768, bytes_accessed=4_000_000, transcendentals=0
        ),
        name="begin",
    )(place, piece, w_out, section, modulation, mlp_cached)


def finish_kernel(place, *refs):
    pieces = refs[: XN - 1]
    w_out, base, gate, out, bufs, result, sems = refs[XN - 1 :]
    me = place[0]
    loads = [
        pltpu.make_async_copy(piece, bufs.at[index], sems.at[index])
        for index, piece in enumerate(pieces)
    ]
    for load in loads:
        load.start()
    starts = [
        pl.multiple_of(lax.rem(me - shift + XN, XN) * WH, WH) for shift in (3, 1, 2)
    ]
    stores = []
    for part, cols in enumerate((slice(0, 512), slice(512, 768))):
        total = None
        for index, start in enumerate(starts):
            if part == 0:
                loads[index].wait()
            product = jnp.dot(
                bufs[index], w_out[pl.ds(start, WH), cols], preferred_element_type=f32
            )
            total = product if total is None else total + product
        result[:, cols] = (base[:, cols] + gate[:, cols] * total).astype(bf16)
        stores.append(
            pltpu.make_async_copy(result.at[:, cols], out.at[:, cols], sems.at[XN - 1 + part])
        )
        stores[part].start()
    for store in stores:
        store.wait()


def finish(place, pieces, w_out, total, gate):
    vmem = pl.BlockSpec(memory_space=pltpu.VMEM)
    any_spec = pl.BlockSpec(memory_space=pl.ANY)
    return pl.pallas_call(
        finish_kernel,
        out_shape=jax.ShapeDtypeStruct(total.shape, bf16),
        in_specs=[pl.BlockSpec(memory_space=pltpu.SMEM)] + [any_spec] * (XN - 1) + [vmem] * 3,
        out_specs=any_spec,
        scratch_shapes=[
            pltpu.VMEM((XN - 1, SEC, WH), bf16),
            pltpu.VMEM(total.shape, bf16),
            pltpu.SemaphoreType.DMA((XN + 1,)),
        ],
        compiler_params=pltpu.CompilerParams(vmem_limit_bytes=SMALL_VMEM),
        cost_estimate=pl.CostEstimate(
            flops=2 * SEC * (XN - 1) * WH * 768, bytes_accessed=3_000_000, transcendentals=0
        ),
        name="finish",
    )(place, *pieces, w_out, total, gate)


def seq_send(array, target_of):
    pairs = []
    for z in range(ZN):
        for y in range(YN):
            for c in range(CN):
                tz, ty, tc = target_of(z, y, c)
                target = (tz % ZN * YN + ty % YN) * CN + tc % CN
                pairs.append(((z * YN + y) * CN + c, target))
    return lax.ppermute(array, "seq", pairs)


def ring(array):
    return seq_send(array, lambda z, y, c: (z + 1 - 2 * c, y, c))


def swap(array):
    return seq_send(array, lambda z, y, c: (z, y, c + 1))


def after(array, others):
    return lax.optimization_barrier((array, others))[0]


def y_shift(array, dy):
    return seq_send(array, lambda z, y, c: (z, y + dy, c))


def tp_shift(array, dx):
    return lax.ppermute(array, "tp", [(x, (x + dx) % XN) for x in range(XN)])


def local(section, history, levels, mlp_cached, w_qkv, w_out, modulation, level_embed):
    key_value, query = prep(section, history, levels, w_qkv, modulation, level_embed)
    first, second = [key_value], [swap(key_value)]
    first.append(ring(first[0]))
    second.append(ring(second[0]))
    queries = [y_shift(after(query, second[0]), 1)] + [y_shift(query, dy) for dy in (2, 3)]
    query, first[0] = stage(query, key_value)
    first[1] = after(first[1], (queries[0], queries[2], query, first[0]))
    first.append(ring(first[1]))
    second.append(ring(second[1]))
    first[2] = after(first[2], queries[1])
    first.append(ring(first[2]))
    queries = [query] + queries
    state = attend(queries, [first[0], second[0], first[1], second[1]], None, False)
    others = [swap(chunk) for chunk in (first[1], second[1])]
    second[2] = after(second[2], state)
    second.append(ring(second[2]))
    first[3] = after(first[3], state)
    first.append(ring(first[3]))
    others_2 = [swap(chunk) for chunk in (after(first[2], state), second[2])]
    state = attend(queries, others + [first[2], second[2]], state, False)
    others = [swap(after(chunk, state)) for chunk in (first[3], second[3])]
    state = attend(queries, others_2 + [first[3], second[3]], state, False)
    first[4] = after(first[4], state)
    state = attend(queries, others, state, False)
    parts = attend(queries, [first[4], swap(first[4])], state, True)
    sent = [y_shift(parts[dy], -dy) for dy in (2, 1, 3)]
    attended = merge([parts[0]] + sent)
    place = lax.axis_index("tp").astype(jnp.int32).reshape(1)
    pieces = [tp_shift(attended, dx) for dx in (3, 1, 2)]
    total, gate = begin(place, attended, w_out, section, modulation, mlp_cached)
    return finish(place, pieces, w_out, total, gate)


def solution(mesh):
    return jax.shard_map(
        local,
        mesh=mesh,
        in_specs=(
            P("seq", None),
            P("seq", None),
            P("seq"),
            P("seq", "tp"),
            P(None, None, "tp"),
            P(None, "tp"),
            P(),
            P(),
        ),
        out_specs=P("seq", "tp"),
        check_vma=False,
    )
```

```python
import functools
import math

import jax
import jax.numpy as jnp
from jax import lax
from jax.experimental import pallas as pl
from jax.experimental.pallas import tpu as pltpu
from jax.sharding import PartitionSpec as P

HD = 128
HEADS_DEV = 3
WH = HEADS_DEV * HD
D = 3072
ZN, YN, CN, XN = 8, 4, 2, 4
SEC = 128
CTX = 64
ROWS = SEC + CTX
FT = 64
FRAMES = 4
STAT_ROWS = 16
PAD_KEY = 2.0**126
PAD_TEST = 2.0**125
TO_LOG2 = HD**-0.5 * math.log2(math.e)
MIB = 1024 * 1024
PREP_VMEM = 63 * MIB
ATTEND_VMEM = 24 * MIB
SMALL_VMEM = 8 * MIB

f32 = jnp.float32
bf16 = jnp.bfloat16


def norm_rows(rows, shift_row, scale_row):
    row_mean = jnp.mean(rows, axis=-1, keepdims=True)
    centred = rows - row_mean
    spread = jnp.mean(centred * centred, axis=-1, keepdims=True)
    return (centred * lax.rsqrt(spread + 1e-06) * (1.0 + scale_row) + shift_row).astype(bf16)


def prep_kernel(
    levels_in, modulation_in, embed_in, section, history, w_qkv,
    key_value, queries,
    levels, modulation, level_embed, sec_buf, hist_buf, w_buf, pooled, rows_h, sems,
):
    half = D // 2
    spans = [pl.ds(0, half), pl.ds(half, half)]
    copies = [
        pltpu.make_async_copy(levels_in, levels, sems.at[0]),
        pltpu.make_async_copy(modulation_in, modulation, sems.at[1]),
        pltpu.make_async_copy(section, sec_buf, sems.at[2]),
        pltpu.make_async_copy(history, hist_buf, sems.at[3]),
        pltpu.make_async_copy(embed_in, level_embed, sems.at[4]),
    ]
    weight_copies = [
        pltpu.make_async_copy(
            w_qkv.at[which, spans[part]],
            w_buf.at[spans[part], pl.ds(place * WH, WH)],
            sems.at[5 + index],
        )
        for index, (which, place, part) in enumerate(
            ((0, 2, 0), (0, 2, 1), (1, 0, 0), (2, 1, 0), (1, 0, 1), (2, 1, 1))
        )
    ]
    for copy in copies[:3] + weight_copies[:2] + copies[3:] + weight_copies[2:]:
        copy.start()

    copies[1].wait()
    shift_row = modulation[0:1, :]
    scale_row = modulation[1:2, :]
    copies[2].wait()

    def section_step(step, carry):
        span = pl.ds(pl.multiple_of(step * 16, 16), 16)
        rows_h[span, :] = norm_rows(sec_buf[span, :].astype(f32), shift_row, scale_row)
        return carry

    lax.fori_loop(0, SEC // 16, section_step, 0, unroll=4)

    copies[0].wait()
    counts = []
    starts = []
    total = jnp.int32(0)
    for frame in range(FRAMES):
        starts.append(total)
        counts.append(lax.shift_right_logical(jnp.int32(FT // 2), levels[frame]))
        total = total + counts[frame]

    slot = lax.broadcasted_iota(jnp.int32, (CTX, FRAMES * FT), 0)
    source = lax.broadcasted_iota(jnp.int32, (CTX, FRAMES * FT), 1)
    factors = jnp.zeros((CTX, FRAMES * FT), f32)
    for frame in range(FRAMES):
        width = lax.shift_left(jnp.int32(2), levels[frame])
        first = (slot - starts[frame]) * width + frame * FT
        inside = (
            (source >= first)
            & (source < first + width)
            & (source >= frame * FT)
            & (source < (frame + 1) * FT)
        )
        factors = factors + jnp.where(inside, 1.0 / width.astype(f32), 0.0)
    copies[3].wait()
    pooled[...] = jnp.dot(factors.astype(bf16), hist_buf[...], preferred_element_type=f32)
    copies[4].wait()

    weight_copies[0].wait()
    weight_copies[1].wait()
    asked = jnp.dot(rows_h[:SEC, :], w_buf[:, 2 * WH :], preferred_element_type=f32)
    for step in range(CTX // 16):
        span = slice(step * 16, (step + 1) * 16)
        rows = pooled[span, :]
        index = lax.broadcasted_iota(jnp.int32, (16, 1), 0) + step * 16
        for frame in range(FRAMES):
            mine = (index >= starts[frame]) & (index < starts[frame] + counts[frame])
            rows = rows + jnp.where(mine, level_embed[pl.ds(levels[frame], 1), :], 0.0)
        rows_h[SEC + step * 16 : SEC + (step + 1) * 16, :] = norm_rows(
            rows, shift_row, scale_row
        )
    queries[...] = (asked * TO_LOG2).astype(bf16)

    both = None
    for part in range(2):
        weight_copies[2 + 2 * part].wait()
        weight_copies[3 + 2 * part].wait()
        span = slice(part * half, (part + 1) * half)
        piece = jnp.dot(
            rows_h[:, span], w_buf[span, : 2 * WH], preferred_element_type=f32
        )
        both = piece if part == 0 else both + piece
    row_index = lax.broadcasted_iota(jnp.int32, (ROWS, WH), 0)
    key_value[0] = jnp.where(row_index < SEC + total, both[:, :WH], PAD_KEY).astype(bf16)
    key_value[1] = both[:, WH:].astype(bf16)


def prep(section, history, levels, w_qkv, modulation, level_embed):
    any_spec = pl.BlockSpec(memory_space=pl.ANY)
    vmem = pl.BlockSpec(memory_space=pltpu.VMEM)
    return pl.pallas_call(
        prep_kernel,
        out_shape=(
            jax.ShapeDtypeStruct((2, ROWS, WH), bf16),
            jax.ShapeDtypeStruct((SEC, WH), bf16),
        ),
        in_specs=[any_spec] * 6,
        out_specs=(vmem, vmem),
        scratch_shapes=[
            pltpu.SMEM((FRAMES,), jnp.int32),
            pltpu.VMEM((3, D), f32),
            pltpu.VMEM((4, D), f32),
            pltpu.VMEM((SEC, D), bf16),
            pltpu.VMEM((FRAMES * FT, D), bf16),
            pltpu.VMEM((D, 3 * WH), bf16),
            pltpu.VMEM((CTX, D), f32),
            pltpu.VMEM((ROWS, D), bf16),
            pltpu.SemaphoreType.DMA((11,)),
        ],
        compiler_params=pltpu.CompilerParams(vmem_limit_bytes=PREP_VMEM),
        cost_estimate=pl.CostEstimate(
            flops=2 * ROWS * D * 3 * WH, bytes_accessed=12_000_000, transcendentals=0
        ),
        name="prep",
    )(levels, modulation, level_embed, section, history, w_qkv)


def stage_kernel(query_in, block_in, query, block, sems):
    copies = [
        pltpu.make_async_copy(query_in, query, sems.at[0]),
        pltpu.make_async_copy(block_in, block, sems.at[1]),
    ]
    for copy in copies:
        copy.start()
    for copy in copies:
        copy.wait()


def stage(query, block):
    any_spec = pl.BlockSpec(memory_space=pl.ANY)
    vmem = pl.BlockSpec(memory_space=pltpu.VMEM)
    return pl.pallas_call(
        stage_kernel,
        out_shape=(
            jax.ShapeDtypeStruct(query.shape, bf16),
            jax.ShapeDtypeStruct(block.shape, bf16),
        ),
        in_specs=[any_spec, any_spec],
        out_specs=(vmem, vmem),
        scratch_shapes=[pltpu.SemaphoreType.DMA((2,))],
        compiler_params=pltpu.CompilerParams(vmem_limit_bytes=SMALL_VMEM),
        cost_estimate=pl.CostEstimate(flops=0, bytes_accessed=800_000, transcendentals=0),
        name="stage",
    )(query, block)


def attend_kernel(block_shapes, first, last, *refs):
    refs = list(refs)
    query_refs = [refs.pop(0) for _ in range(YN)]
    blocks = []
    for joint in block_shapes:
        if joint:
            ref = refs.pop(0)
            blocks.append((ref.at[0], ref.at[1]))
        else:
            key_ref = refs.pop(0)
            blocks.append((key_ref, refs.pop(0)))
    if not first:
        max_in, den_in, num_in = refs.pop(0), refs.pop(0), refs.pop(0)
    outs = refs
    pad = [key_ref[SEC:ROWS, 0:1].astype(f32) > PAD_TEST for key_ref, _ in blocks]

    joint = 2 if len(blocks) == 2 else 1

    def all_scores(head, pair):
        cols = slice(head * HD, (head + 1) * HD)
        query = jnp.concatenate(
            [query_refs[2 * pair][:, cols], query_refs[2 * pair + 1][:, cols]], axis=0
        )
        scores = []
        for start in range(0, len(blocks), joint):
            keys = jnp.concatenate([ref[:, cols] for ref, _ in blocks[start : start + joint]], axis=0)
            whole = lax.dot_general(
                keys, query, (((1,), (1,)), ((), ())), preferred_element_type=f32
            )
            for index, pad_rows in enumerate(pad[start : start + joint]):
                score = whole[index * ROWS : (index + 1) * ROWS]
                scores.append(score[:SEC])
                scores.append(jnp.where(pad_rows, -1e30, score[SEC:]))
        return scores

    order = [(head, pair) for head in range(HEADS_DEV) for pair in range(YN // 2)]
    coming = all_scores(*order[0])
    for place, (head, pair) in enumerate(order):
        cols = slice(head * HD, (head + 1) * HD)
        lanes = slice(pair * 2 * SEC, (pair + 1) * 2 * SEC)
        scores = coming
        if place + 1 < len(order):
            coming = all_scores(*order[place + 1])
        if True:
            new_max = functools.reduce(
                jnp.maximum, [jnp.max(score, axis=0, keepdims=True) for score in scores]
            )
            if not first:
                old_max = max_in[head : head + 1, lanes]
                new_max = jnp.maximum(new_max, old_max)
                rescale = jnp.exp2(old_max - new_max)
                denominator = den_in[head : head + 1, lanes] * rescale
                numerator = num_in[cols, lanes] * rescale
            else:
                denominator = jnp.zeros((1, 2 * SEC), f32)
                numerator = jnp.zeros((HD, 2 * SEC), f32)
            for start in range(0, len(blocks), joint):
                expon = [
                    jnp.exp2(score - new_max)
                    for score in scores[2 * start : 2 * (start + joint)]
                ]
                for part in expon:
                    denominator = denominator + jnp.sum(part, axis=0, keepdims=True)
                weights = jnp.concatenate([part.astype(bf16) for part in expon], axis=0)
                values = jnp.concatenate(
                    [ref[:, cols] for _, ref in blocks[start : start + joint]], axis=0
                )
                numerator = numerator + lax.dot_general(
                    values, weights, (((0,), (0,)), ((), ())), preferred_element_type=f32
                )
            if not last:
                outs[0][head : head + 1, lanes] = new_max
                outs[1][head : head + 1, lanes] = denominator
                outs[2][cols, lanes] = numerator
            else:
                local_out = (numerator / denominator).astype(bf16)
                stat = new_max + jnp.log2(denominator)
                high = stat.astype(bf16).astype(f32)
                middle = (stat - high).astype(bf16).astype(f32)
                low = stat - high - middle
                for half in range(2):
                    piece = slice(half * SEC, (half + 1) * SEC)
                    out = outs[2 * pair + half]
                    out[cols, :] = local_out[:, piece]
                    block = jnp.concatenate(
                        [high[:, piece], middle[:, piece], low[:, piece]], axis=0
                    )
                    stats_ref = outs[YN + 2 * pair + half]
                    stats_ref[head * 3 : head * 3 + 3, :] = block
    if last:
        for index in range(YN):
            stats_ref = outs[YN + index]
            stats_ref[3 * HEADS_DEV : STAT_ROWS, :] = jnp.zeros(
                (STAT_ROWS - 3 * HEADS_DEV, SEC), f32
            )
            outs[index][WH : WH + STAT_ROWS, :] = stats_ref[...].astype(bf16)


def attend(queries, blocks, state, last):
    vmem = pl.BlockSpec(memory_space=pltpu.VMEM)
    block_shapes = tuple(not isinstance(block, tuple) for block in blocks)
    flat = []
    for block in blocks:
        flat.extend(block if isinstance(block, tuple) else (block,))
    operands = list(queries) + flat + (list(state) if state is not None else [])
    count = len(blocks)
    if last:
        out_shape = tuple(
            jax.ShapeDtypeStruct((WH + STAT_ROWS, SEC), bf16) for _ in range(YN)
        )
        scratch = [pltpu.VMEM((STAT_ROWS, SEC), f32) for _ in range(YN)]
    else:
        out_shape = (
            jax.ShapeDtypeStruct((HEADS_DEV, YN * SEC), f32),
            jax.ShapeDtypeStruct((HEADS_DEV, YN * SEC), f32),
            jax.ShapeDtypeStruct((WH, YN * SEC), f32),
        )
        scratch = []
    return pl.pallas_call(
        functools.partial(attend_kernel, block_shapes, state is None, last),
        out_shape=out_shape,
        in_specs=[vmem] * len(operands),
        out_specs=tuple([vmem] * len(out_shape)),
        scratch_shapes=scratch,
        compiler_params=pltpu.CompilerParams(vmem_limit_bytes=ATTEND_VMEM),
        cost_estimate=pl.CostEstimate(
            flops=4 * count * ROWS * YN * SEC * WH,
            bytes_accessed=count * ROWS * WH * 4 + 2_000_000,
            transcendentals=count * ROWS * YN * SEC * HEADS_DEV,
        ),
        name="attend",
    )(*operands)


def merge_kernel(*refs):
    parts, out = refs[:YN], refs[YN]
    for head in range(HEADS_DEV):
        cols = slice(head * HD, (head + 1) * HD)
        stats = []
        for part in parts:
            block = part[WH : WH + STAT_ROWS, :].astype(f32)
            stats.append(
                block[3 * head : 3 * head + 1]
                + block[3 * head + 1 : 3 * head + 2]
                + block[3 * head + 2 : 3 * head + 3]
            )
        top = functools.reduce(jnp.maximum, stats)
        shares = [jnp.exp2(stat - top) for stat in stats]
        whole = functools.reduce(jnp.add, shares)
        total = functools.reduce(
            jnp.add, [part[cols, :].astype(f32) * share for part, share in zip(parts, shares)]
        )
        out[:, cols] = jnp.transpose(total / whole).astype(bf16)


def merge(parts):
    vmem = pl.BlockSpec(memory_space=pltpu.VMEM)
    return pl.pallas_call(
        merge_kernel,
        out_shape=jax.ShapeDtypeStruct((SEC, WH), bf16),
        in_specs=[vmem] * YN,
        out_specs=vmem,
        compiler_params=pltpu.CompilerParams(vmem_limit_bytes=SMALL_VMEM),
        cost_estimate=pl.CostEstimate(flops=500_000, bytes_accessed=500_000, transcendentals=0),
        name="merge",
    )(*parts)


def owned_rows(w_out, owner):
    return w_out[pl.ds(pl.multiple_of(owner * WH, WH), WH), :]


def begin_kernel(place, piece, w_out, section, modulation, mlp, total, gate):
    me = place[0]
    width = total.shape[1]
    cols = pl.ds(pl.multiple_of(me * width, width), width)
    gate[...] = modulation[2:3, cols]
    product = jnp.dot(piece[...], owned_rows(w_out, me), preferred_element_type=f32)
    total[...] = section[:, cols].astype(f32) + gate[...] * (product + mlp[...].astype(f32))


def begin(place, piece, w_out, section, modulation, mlp_cached):
    vmem = pl.BlockSpec(memory_space=pltpu.VMEM)
    return pl.pallas_call(
        begin_kernel,
        out_shape=(
            jax.ShapeDtypeStruct(mlp_cached.shape, f32),
            jax.ShapeDtypeStruct((1, mlp_cached.shape[1]), f32),
        ),
        in_specs=[pl.BlockSpec(memory_space=pltpu.SMEM)] + [vmem] * 5,
        out_specs=(vmem, vmem),
        compiler_params=pltpu.CompilerParams(vmem_limit_bytes=SMALL_VMEM),
        cost_estimate=pl.CostEstimate(
            flops=2 * SEC * WH * 768, bytes_accessed=4_000_000, transcendentals=0
        ),
        name="begin",
    )(place, piece, w_out, section, modulation, mlp_cached)


def finish_kernel(place, *refs):
    pieces = refs[: XN - 1]
    w_out, base, gate, out, bufs, result, sems = refs[XN - 1 :]
    me = place[0]
    loads = [
        pltpu.make_async_copy(piece, bufs.at[index], sems.at[index])
        for index, piece in enumerate(pieces)
    ]
    for load in loads:
        load.start()
    starts = [
        pl.multiple_of(lax.rem(me - shift + XN, XN) * WH, WH) for shift in (3, 1, 2)
    ]
    stores = []
    for part, cols in enumerate((slice(0, 512), slice(512, 768))):
        total = None
        for index, start in enumerate(starts):
            if part == 0:
                loads[index].wait()
            product = jnp.dot(
                bufs[index], w_out[pl.ds(start, WH), cols], preferred_element_type=f32
            )
            total = product if total is None else total + product
        result[:, cols] = (base[:, cols] + gate[:, cols] * total).astype(bf16)
        stores.append(
            pltpu.make_async_copy(result.at[:, cols], out.at[:, cols], sems.at[XN - 1 + part])
        )
        stores[part].start()
    for store in stores:
        store.wait()


def finish(place, pieces, w_out, total, gate):
    vmem = pl.BlockSpec(memory_space=pltpu.VMEM)
    any_spec = pl.BlockSpec(memory_space=pl.ANY)
    return pl.pallas_call(
        finish_kernel,
        out_shape=jax.ShapeDtypeStruct(total.shape, bf16),
        in_specs=[pl.BlockSpec(memory_space=pltpu.SMEM)] + [any_spec] * (XN - 1) + [vmem] * 3,
        out_specs=any_spec,
        scratch_shapes=[
            pltpu.VMEM((XN - 1, SEC, WH), bf16),
            pltpu.VMEM(total.shape, bf16),
            pltpu.SemaphoreType.DMA((XN + 1,)),
        ],
        compiler_params=pltpu.CompilerParams(vmem_limit_bytes=SMALL_VMEM),
        cost_estimate=pl.CostEstimate(
            flops=2 * SEC * (XN - 1) * WH * 768, bytes_accessed=3_000_000, transcendentals=0
        ),
        name="finish",
    )(place, *pieces, w_out, total, gate)


def seq_send(array, target_of):
    pairs = []
    for z in range(ZN):
        for y in range(YN):
            for c in range(CN):
                tz, ty, tc = target_of(z, y, c)
                target = (tz % ZN * YN + ty % YN) * CN + tc % CN
                pairs.append(((z * YN + y) * CN + c, target))
    return lax.ppermute(array, "seq", pairs)


def ring(array):
    return seq_send(array, lambda z, y, c: (z + 1 - 2 * c, y, c))


def swap(array):
    return seq_send(array, lambda z, y, c: (z, y, c + 1))


def after(array, others):
    return lax.optimization_barrier((array, others))[0]


def y_shift(array, dy):
    return seq_send(array, lambda z, y, c: (z, y + dy, c))


def tp_shift(array, dx):
    return lax.ppermute(array, "tp", [(x, (x + dx) % XN) for x in range(XN)])


def local(section, history, levels, mlp_cached, w_qkv, w_out, modulation, level_embed):
    key_value, query = prep(section, history, levels, w_qkv, modulation, level_embed)
    first, second = [key_value], [swap(key_value)]
    first.append(ring(first[0]))
    second.append(ring(second[0]))
    queries = [y_shift(after(query, second[0]), 1)] + [y_shift(query, dy) for dy in (2, 3)]
    query, first[0] = stage(query, key_value)
    first[1] = after(first[1], (queries[0], queries[2], query, first[0]))
    first.append(ring(first[1]))
    second.append(ring(second[1]))
    first[2] = after(first[2], queries[1])
    first.append(ring(first[2]))
    queries = [query] + queries
    state = attend(queries, [first[0], second[0], first[1], second[1]], None, False)
    others = [swap(chunk) for chunk in (first[1], second[1])]
    second[2] = after(second[2], state)
    second.append(ring(second[2]))
    first[3] = after(first[3], state)
    first.append(ring(first[3]))
    others_2 = [swap(chunk) for chunk in (after(first[2], state), second[2])]
    state = attend(queries, others + [first[2], second[2]], state, False)
    others = [swap(after(chunk, state)) for chunk in (first[3], second[3])]
    state = attend(queries, others_2 + [first[3], second[3]], state, False)
    first[4] = after(first[4], state)
    state = attend(queries, others, state, False)
    parts = attend(queries, [first[4], swap(first[4])], state, True)
    sent = [y_shift(parts[dy], -dy) for dy in (2, 1, 3)]
    attended = merge([parts[0]] + sent)
    place = lax.axis_index("tp").astype(jnp.int32).reshape(1)
    pieces = [tp_shift(attended, dx) for dx in (3, 1, 2)]
    total, gate = begin(place, attended, w_out, section, modulation, mlp_cached)
    return finish(place, pieces, w_out, total, gate)


def solution(mesh):
    return jax.shard_map(
        local,
        mesh=mesh,
        in_specs=(
            P("seq", None),
            P("seq", None),
            P("seq"),
            P("seq", "tp"),
            P(None, None, "tp"),
            P(None, "tp"),
            P(),
            P(),
        ),
        out_specs=P("seq", "tp"),
        check_vma=False,
    )
```

```python
import functools
import math

import jax
import jax.numpy as jnp
from jax import lax
from jax.experimental import pallas as pl
from jax.experimental.pallas import tpu as pltpu
from jax.sharding import PartitionSpec as P

HD = 128
HEADS_DEV = 3
WH = HEADS_DEV * HD
D = 3072
ZN, YN, CN, XN = 8, 4, 2, 4
SEC = 128
CTX = 64
ROWS = SEC + CTX
FT = 64
FRAMES = 4
STAT_ROWS = 16
PAD_KEY = 2.0**126
PAD_TEST = 2.0**125
TO_LOG2 = HD**-0.5 * math.log2(math.e)
MIB = 1024 * 1024
PREP_VMEM = 63 * MIB
ATTEND_VMEM = 24 * MIB
SMALL_VMEM = 8 * MIB

f32 = jnp.float32
bf16 = jnp.bfloat16


def norm_rows(rows, shift_row, scale_row):
    row_mean = jnp.mean(rows, axis=-1, keepdims=True)
    centred = rows - row_mean
    spread = jnp.mean(centred * centred, axis=-1, keepdims=True)
    return (centred * lax.rsqrt(spread + 1e-06) * (1.0 + scale_row) + shift_row).astype(bf16)


def prep_kernel(
    levels_in, modulation_in, embed_in, section, history, w_qkv,
    key_value, queries,
    levels, modulation, level_embed, sec_buf, hist_buf, w_buf, pooled, rows_h, sems,
):
    half = D // 2
    spans = [pl.ds(0, half), pl.ds(half, half)]
    copies = [
        pltpu.make_async_copy(levels_in, levels, sems.at[0]),
        pltpu.make_async_copy(modulation_in, modulation, sems.at[1]),
        pltpu.make_async_copy(section, sec_buf, sems.at[2]),
        pltpu.make_async_copy(history, hist_buf, sems.at[3]),
        pltpu.make_async_copy(embed_in, level_embed, sems.at[4]),
    ]
    weight_copies = [
        pltpu.make_async_copy(
            w_qkv.at[which, spans[part]],
            w_buf.at[spans[part], pl.ds(place * WH, WH)],
            sems.at[5 + index],
        )
        for index, (which, place, part) in enumerate(
            ((0, 2, 0), (0, 2, 1), (1, 0, 0), (2, 1, 0), (1, 0, 1), (2, 1, 1))
        )
    ]
    for copy in copies[:3] + weight_copies[:2] + copies[3:] + weight_copies[2:]:
        copy.start()

    copies[1].wait()
    shift_row = modulation[0:1, :]
    scale_row = modulation[1:2, :]
    copies[2].wait()

    def section_step(step, carry):
        span = pl.ds(pl.multiple_of(step * 16, 16), 16)
        rows_h[span, :] = norm_rows(sec_buf[span, :].astype(f32), shift_row, scale_row)
        return carry

    lax.fori_loop(0, SEC // 16, section_step, 0, unroll=4)

    copies[0].wait()
    counts = []
    starts = []
    total = jnp.int32(0)
    for frame in range(FRAMES):
        starts.append(total)
        counts.append(lax.shift_right_logical(jnp.int32(FT // 2), levels[frame]))
        total = total + counts[frame]

    slot = lax.broadcasted_iota(jnp.int32, (CTX, FRAMES * FT), 0)
    source = lax.broadcasted_iota(jnp.int32, (CTX, FRAMES * FT), 1)
    factors = jnp.zeros((CTX, FRAMES * FT), f32)
    for frame in range(FRAMES):
        width = lax.shift_left(jnp.int32(2), levels[frame])
        first = (slot - starts[frame]) * width + frame * FT
        inside = (
            (source >= first)
            & (source < first + width)
            & (source >= frame * FT)
            & (source < (frame + 1) * FT)
        )
        factors = factors + jnp.where(inside, 1.0 / width.astype(f32), 0.0)
    copies[3].wait()
    pooled[...] = jnp.dot(factors.astype(bf16), hist_buf[...], preferred_element_type=f32)
    copies[4].wait()

    weight_copies[0].wait()
    weight_copies[1].wait()
    asked = jnp.dot(rows_h[:SEC, :], w_buf[:, 2 * WH :], preferred_element_type=f32)
    for step in range(CTX // 16):
        span = slice(step * 16, (step + 1) * 16)
        rows = pooled[span, :]
        index = lax.broadcasted_iota(jnp.int32, (16, 1), 0) + step * 16
        for frame in range(FRAMES):
            mine = (index >= starts[frame]) & (index < starts[frame] + counts[frame])
            rows = rows + jnp.where(mine, level_embed[pl.ds(levels[frame], 1), :], 0.0)
        rows_h[SEC + step * 16 : SEC + (step + 1) * 16, :] = norm_rows(
            rows, shift_row, scale_row
        )
    queries[...] = (asked * TO_LOG2).astype(bf16)

    both = None
    for part in range(2):
        weight_copies[2 + 2 * part].wait()
        weight_copies[3 + 2 * part].wait()
        span = slice(part * half, (part + 1) * half)
        piece = jnp.dot(
            rows_h[:, span], w_buf[span, : 2 * WH], preferred_element_type=f32
        )
        both = piece if part == 0 else both + piece
    row_index = lax.broadcasted_iota(jnp.int32, (ROWS, WH), 0)
    key_value[0] = jnp.where(row_index < SEC + total, both[:, :WH], PAD_KEY).astype(bf16)
    key_value[1] = both[:, WH:].astype(bf16)


def prep(section, history, levels, w_qkv, modulation, level_embed):
    any_spec = pl.BlockSpec(memory_space=pl.ANY)
    vmem = pl.BlockSpec(memory_space=pltpu.VMEM)
    return pl.pallas_call(
        prep_kernel,
        out_shape=(
            jax.ShapeDtypeStruct((2, ROWS, WH), bf16),
            jax.ShapeDtypeStruct((SEC, WH), bf16),
        ),
        in_specs=[any_spec] * 6,
        out_specs=(vmem, vmem),
        scratch_shapes=[
            pltpu.SMEM((FRAMES,), jnp.int32),
            pltpu.VMEM((3, D), f32),
            pltpu.VMEM((4, D), f32),
            pltpu.VMEM((SEC, D), bf16),
            pltpu.VMEM((FRAMES * FT, D), bf16),
            pltpu.VMEM((D, 3 * WH), bf16),
            pltpu.VMEM((CTX, D), f32),
            pltpu.VMEM((ROWS, D), bf16),
            pltpu.SemaphoreType.DMA((11,)),
        ],
        compiler_params=pltpu.CompilerParams(vmem_limit_bytes=PREP_VMEM),
        cost_estimate=pl.CostEstimate(
            flops=2 * ROWS * D * 3 * WH, bytes_accessed=12_000_000, transcendentals=0
        ),
        name="prep",
    )(levels, modulation, level_embed, section, history, w_qkv)


def stage_kernel(query_in, block_in, query, block, sems):
    copies = [
        pltpu.make_async_copy(query_in, query, sems.at[0]),
        pltpu.make_async_copy(block_in, block, sems.at[1]),
    ]
    for copy in copies:
        copy.start()
    for copy in copies:
        copy.wait()


def stage(query, block):
    any_spec = pl.BlockSpec(memory_space=pl.ANY)
    vmem = pl.BlockSpec(memory_space=pltpu.VMEM)
    return pl.pallas_call(
        stage_kernel,
        out_shape=(
            jax.ShapeDtypeStruct(query.shape, bf16),
            jax.ShapeDtypeStruct(block.shape, bf16),
        ),
        in_specs=[any_spec, any_spec],
        out_specs=(vmem, vmem),
        scratch_shapes=[pltpu.SemaphoreType.DMA((2,))],
        compiler_params=pltpu.CompilerParams(vmem_limit_bytes=SMALL_VMEM),
        cost_estimate=pl.CostEstimate(flops=0, bytes_accessed=800_000, transcendentals=0),
        name="stage",
    )(query, block)


def attend_kernel(block_shapes, first, last, *refs):
    refs = list(refs)
    query_refs = [refs.pop(0) for _ in range(YN)]
    blocks = []
    for joint in block_shapes:
        if joint:
            ref = refs.pop(0)
            blocks.append((ref.at[0], ref.at[1]))
        else:
            key_ref = refs.pop(0)
            blocks.append((key_ref, refs.pop(0)))
    if not first:
        max_in, den_in, num_in = refs.pop(0), refs.pop(0), refs.pop(0)
    outs = refs
    pad = [key_ref[SEC:ROWS, 0:1].astype(f32) > PAD_TEST for key_ref, _ in blocks]

    def all_scores(head, pair):
        cols = slice(head * HD, (head + 1) * HD)
        query = jnp.concatenate(
            [query_refs[2 * pair][:, cols], query_refs[2 * pair + 1][:, cols]], axis=0
        )
        scores = []
        for (key_ref, _), pad_rows in zip(blocks, pad):
            score = lax.dot_general(
                key_ref[:, cols], query, (((1,), (1,)), ((), ())), preferred_element_type=f32
            )
            scores.append(score[:SEC])
            scores.append(jnp.where(pad_rows, -1e30, score[SEC:]))
        return scores

    order = [(head, pair) for head in range(HEADS_DEV) for pair in range(YN // 2)]
    coming = all_scores(*order[0])
    for place, (head, pair) in enumerate(order):
        cols = slice(head * HD, (head + 1) * HD)
        lanes = slice(pair * 2 * SEC, (pair + 1) * 2 * SEC)
        scores = coming
        if place + 1 < len(order):
            coming = all_scores(*order[place + 1])
        if True:
            new_max = functools.reduce(
                jnp.maximum, [jnp.max(score, axis=0, keepdims=True) for score in scores]
            )
            if not first:
                old_max = max_in[head : head + 1, lanes]
                new_max = jnp.maximum(new_max, old_max)
                rescale = jnp.exp2(old_max - new_max)
                denominator = den_in[head : head + 1, lanes] * rescale
                numerator = num_in[cols, lanes] * rescale
            else:
                denominator = jnp.zeros((1, 2 * SEC), f32)
                numerator = jnp.zeros((HD, 2 * SEC), f32)
            for index, (_, value_ref) in enumerate(blocks):
                expon = [
                    jnp.exp2(score - new_max) for score in scores[2 * index : 2 * index + 2]
                ]
                for part in expon:
                    denominator = denominator + jnp.sum(part, axis=0, keepdims=True)
                weights = jnp.concatenate([part.astype(bf16) for part in expon], axis=0)
                numerator = numerator + lax.dot_general(
                    value_ref[:, cols], weights, (((0,), (0,)), ((), ())),
                    preferred_element_type=f32,
                )
            if not last:
                outs[0][head : head + 1, lanes] = new_max
                outs[1][head : head + 1, lanes] = denominator
                outs[2][cols, lanes] = numerator
            else:
                local_out = (numerator / denominator).astype(bf16)
                stat = new_max + jnp.log2(denominator)
                high = stat.astype(bf16).astype(f32)
                middle = (stat - high).astype(bf16).astype(f32)
                low = stat - high - middle
                for half in range(2):
                    piece = slice(half * SEC, (half + 1) * SEC)
                    out = outs[2 * pair + half]
                    out[cols, :] = local_out[:, piece]
                    block = jnp.concatenate(
                        [high[:, piece], middle[:, piece], low[:, piece]], axis=0
                    )
                    stats_ref = outs[YN + 2 * pair + half]
                    stats_ref[head * 3 : head * 3 + 3, :] = block
    if last:
        for index in range(YN):
            stats_ref = outs[YN + index]
            stats_ref[3 * HEADS_DEV : STAT_ROWS, :] = jnp.zeros(
                (STAT_ROWS - 3 * HEADS_DEV, SEC), f32
            )
            outs[index][WH : WH + STAT_ROWS, :] = stats_ref[...].astype(bf16)


def attend(queries, blocks, state, last):
    vmem = pl.BlockSpec(memory_space=pltpu.VMEM)
    block_shapes = tuple(not isinstance(block, tuple) for block in blocks)
    flat = []
    for block in blocks:
        flat.extend(block if isinstance(block, tuple) else (block,))
    operands = list(queries) + flat + (list(state) if state is not None else [])
    count = len(blocks)
    if last:
        out_shape = tuple(
            jax.ShapeDtypeStruct((WH + STAT_ROWS, SEC), bf16) for _ in range(YN)
        )
        scratch = [pltpu.VMEM((STAT_ROWS, SEC), f32) for _ in range(YN)]
    else:
        out_shape = (
            jax.ShapeDtypeStruct((HEADS_DEV, YN * SEC), f32),
            jax.ShapeDtypeStruct((HEADS_DEV, YN * SEC), f32),
            jax.ShapeDtypeStruct((WH, YN * SEC), f32),
        )
        scratch = []
    return pl.pallas_call(
        functools.partial(attend_kernel, block_shapes, state is None, last),
        out_shape=out_shape,
        in_specs=[vmem] * len(operands),
        out_specs=tuple([vmem] * len(out_shape)),
        scratch_shapes=scratch,
        compiler_params=pltpu.CompilerParams(vmem_limit_bytes=ATTEND_VMEM),
        cost_estimate=pl.CostEstimate(
            flops=4 * count * ROWS * YN * SEC * WH,
            bytes_accessed=count * ROWS * WH * 4 + 2_000_000,
            transcendentals=count * ROWS * YN * SEC * HEADS_DEV,
        ),
        name="attend",
    )(*operands)


def merge_kernel(*refs):
    parts, out = refs[:YN], refs[YN]
    for head in range(HEADS_DEV):
        cols = slice(head * HD, (head + 1) * HD)
        stats = []
        for part in parts:
            block = part[WH : WH + STAT_ROWS, :].astype(f32)
            stats.append(
                block[3 * head : 3 * head + 1]
                + block[3 * head + 1 : 3 * head + 2]
                + block[3 * head + 2 : 3 * head + 3]
            )
        top = functools.reduce(jnp.maximum, stats)
        shares = [jnp.exp2(stat - top) for stat in stats]
        whole = functools.reduce(jnp.add, shares)
        total = functools.reduce(
            jnp.add, [part[cols, :].astype(f32) * share for part, share in zip(parts, shares)]
        )
        out[:, cols] = jnp.transpose(total / whole).astype(bf16)


def merge(parts):
    vmem = pl.BlockSpec(memory_space=pltpu.VMEM)
    return pl.pallas_call(
        merge_kernel,
        out_shape=jax.ShapeDtypeStruct((SEC, WH), bf16),
        in_specs=[vmem] * YN,
        out_specs=vmem,
        compiler_params=pltpu.CompilerParams(vmem_limit_bytes=SMALL_VMEM),
        cost_estimate=pl.CostEstimate(flops=500_000, bytes_accessed=500_000, transcendentals=0),
        name="merge",
    )(*parts)


def owned_rows(w_out, owner):
    return w_out[pl.ds(pl.multiple_of(owner * WH, WH), WH), :]


def begin_kernel(place, piece, w_out, section, modulation, mlp, total, gate):
    me = place[0]
    width = total.shape[1]
    cols = pl.ds(pl.multiple_of(me * width, width), width)
    gate[...] = modulation[2:3, cols]
    product = jnp.dot(piece[...], owned_rows(w_out, me), preferred_element_type=f32)
    total[...] = section[:, cols].astype(f32) + gate[...] * (product + mlp[...].astype(f32))


def begin(place, piece, w_out, section, modulation, mlp_cached):
    vmem = pl.BlockSpec(memory_space=pltpu.VMEM)
    return pl.pallas_call(
        begin_kernel,
        out_shape=(
            jax.ShapeDtypeStruct(mlp_cached.shape, f32),
            jax.ShapeDtypeStruct((1, mlp_cached.shape[1]), f32),
        ),
        in_specs=[pl.BlockSpec(memory_space=pltpu.SMEM)] + [vmem] * 5,
        out_specs=(vmem, vmem),
        compiler_params=pltpu.CompilerParams(vmem_limit_bytes=SMALL_VMEM),
        cost_estimate=pl.CostEstimate(
            flops=2 * SEC * WH * 768, bytes_accessed=4_000_000, transcendentals=0
        ),
        name="begin",
    )(place, piece, w_out, section, modulation, mlp_cached)


def finish_kernel(place, *refs):
    pieces = refs[: XN - 1]
    w_out, base, gate, out = refs[XN - 1 :]
    me = place[0]
    products = [
        jnp.dot(
            piece[...],
            owned_rows(w_out, lax.rem(me - shift + XN, XN)),
            preferred_element_type=f32,
        )
        for shift, piece in zip((3, 1, 2), pieces)
    ]
    total = products[0] + products[1] + products[2]
    out[...] = (base[...] + gate[...] * total).astype(bf16)


def finish(place, pieces, w_out, total, gate):
    vmem = pl.BlockSpec(memory_space=pltpu.VMEM)
    return pl.pallas_call(
        finish_kernel,
        out_shape=jax.ShapeDtypeStruct(total.shape, bf16),
        in_specs=[pl.BlockSpec(memory_space=pltpu.SMEM)] + [vmem] * (XN + 2),
        out_specs=vmem,
        compiler_params=pltpu.CompilerParams(vmem_limit_bytes=SMALL_VMEM),
        cost_estimate=pl.CostEstimate(
            flops=2 * SEC * (XN - 1) * WH * 768, bytes_accessed=3_000_000, transcendentals=0
        ),
        name="finish",
    )(place, *pieces, w_out, total, gate)


def seq_send(array, target_of):
    pairs = []
    for z in range(ZN):
        for y in range(YN):
            for c in range(CN):
                tz, ty, tc = target_of(z, y, c)
                target = (tz % ZN * YN + ty % YN) * CN + tc % CN
                pairs.append(((z * YN + y) * CN + c, target))
    return lax.ppermute(array, "seq", pairs)


def ring(array):
    return seq_send(array, lambda z, y, c: (z + 1 - 2 * c, y, c))


def swap(array):
    return seq_send(array, lambda z, y, c: (z, y, c + 1))


def after(array, others):
    return lax.optimization_barrier((array, others))[0]


def y_shift(array, dy):
    return seq_send(array, lambda z, y, c: (z, y + dy, c))


def tp_shift(array, dx):
    return lax.ppermute(array, "tp", [(x, (x + dx) % XN) for x in range(XN)])


def local(section, history, levels, mlp_cached, w_qkv, w_out, modulation, level_embed):
    key_value, query = prep(section, history, levels, w_qkv, modulation, level_embed)
    first, second = [key_value], [swap(key_value)]
    first.append(ring(first[0]))
    second.append(ring(second[0]))
    queries = [y_shift(after(query, second[0]), 1)] + [y_shift(query, dy) for dy in (2, 3)]
    query, first[0] = stage(query, key_value)
    first[1] = after(first[1], (queries[0], queries[2], query, first[0]))
    first.append(ring(first[1]))
    second.append(ring(second[1]))
    first[2] = after(first[2], queries[1])
    first.append(ring(first[2]))
    queries = [query] + queries
    state = attend(queries, [first[0], second[0], first[1], second[1]], None, False)
    others = [swap(chunk) for chunk in (first[1], second[1])]
    second[2] = after(second[2], state)
    second.append(ring(second[2]))
    first[3] = after(first[3], state)
    first.append(ring(first[3]))
    others_2 = [swap(chunk) for chunk in (after(first[2], state), second[2])]
    state = attend(queries, others + [first[2], second[2]], state, False)
    others = [swap(after(chunk, state)) for chunk in (first[3], second[3])]
    state = attend(queries, others_2 + [first[3], second[3]], state, False)
    first[4] = after(first[4], state)
    state = attend(queries, others, state, False)
    parts = attend(queries, [first[4], swap(first[4])], state, True)
    sent = [y_shift(parts[dy], -dy) for dy in (2, 1, 3)]
    attended = merge([parts[0]] + sent)
    place = lax.axis_index("tp").astype(jnp.int32).reshape(1)
    pieces = [tp_shift(attended, dx) for dx in (3, 1, 2)]
    total, gate = begin(place, attended, w_out, section, modulation, mlp_cached)
    return finish(place, pieces, w_out, total, gate)


def solution(mesh):
    return jax.shard_map(
        local,
        mesh=mesh,
        in_specs=(
            P("seq", None),
            P("seq", None),
            P("seq"),
            P("seq", "tp"),
            P(None, None, "tp"),
            P(None, "tp"),
            P(),
            P(),
        ),
        out_specs=P("seq", "tp"),
        check_vma=False,
    )
```
